256 devices in a mesh: outer: 32 (over z, x_lo, core), inner: 8 (over y, x_hi).
Axes of the slice: x: 4 (x_hi: 2, x_lo: 2; x = x_hi * 2 + x_lo), y: 4, z: 8, core: 2. Of those that a mesh axis runs over, the one named last changes fastest.
Arguments:
- query: bfloat16 [131072, 512], P(('outer', 'inner')), may hold values from -28 to 28
- keys: bfloat16 [131072, 512], P(('outer', 'inner')), may hold values from -28 to 28
- values: bfloat16 [131072, 512], P(('outer', 'inner')), may hold values from -6 to 6
- grad_out: bfloat16 [131072, 512], P(('outer', 'inner')), may hold values from -30 to 30
- band: int32 [512, 5], P(('outer', 'inner')), may hold values from -1 to 511, as said below
- prefix_len: int32 [1], replicated, may hold values from 256 to 512
Outputs:
- attended: bfloat16 [131072, 512], P(('outer', 'inner'))
- grad_query: bfloat16 [131072, 512], P(('outer', 'inner'))
- grad_keys: bfloat16 [131072, 512], P(('outer', 'inner'))
- grad_values: bfloat16 [131072, 512], P(('outer', 'inner'))
The draws below stay inside these ranges and needn't reach their ends.
Inputs may be any that keep to these rules, and one draw needn't show every extreme that they name: `band`: row b lists in slot s either block b - 2 + s or -1; the listed blocks form a run that always holds b itself, with lengths of the run before and after b drawn independently from 0 to 2.
All inputs are finite; a program needn't handle non-finite values.
Results may differ from the reference program's by a relative error of at most 0.025.
Values may be sent and summed in bfloat16 or wider, within the bound.
A program may use at most 128 MiB of HBM per device.

```python
import jax
import jax.numpy as jnp
from jax import lax

HEADS = 8
HEAD = 64
F_DEV = 512
PRE = 512
REACH = 2
WIDTH = 512
BLK = 256
FRAMES = 131072
NBLK = 512
N_OUTER = 32
N_INNER = 8


def draw_query(key, part):
    key = jax.random.fold_in(key, 21)
    result = jnp.clip(jax.random.normal(key, (FRAMES, WIDTH), jnp.float32), -5.0, 5.0)
    return result.astype(jnp.bfloat16)


def draw_keys(key, part):
    key = jax.random.fold_in(key, 33)
    result = jnp.clip(jax.random.normal(key, (FRAMES, WIDTH), jnp.float32), -5.0, 5.0)
    return result.astype(jnp.bfloat16)


def draw_grad_out(key, part):
    key = jax.random.fold_in(key, 59)
    base = jnp.clip(jax.random.normal(key, (FRAMES, WIDTH), jnp.float32), -6.0, 6.0)
    frame = jnp.arange(FRAMES, dtype=jnp.float32)
    center = float(FRAMES // 2 + F_DEV // 2)
    spread = float(FRAMES) / 32.0
    bump = 1.0 + 4.0 * jnp.exp(-((frame - center) / spread) ** 2)
    return (base * bump[:, None]).astype(jnp.bfloat16)


def draw_band(key, part):
    key = jax.random.fold_in(key, 47)
    first, second = jax.random.split(key)
    lower = jax.random.randint(first, (NBLK, 1), 0, REACH + 1)
    upper = jax.random.randint(second, (NBLK, 1), 0, REACH + 1)
    block = jnp.arange(NBLK, dtype=jnp.int32)[:, None]
    offset = jnp.arange(2 * REACH + 1, dtype=jnp.int32)[None, :] - REACH
    target = block + offset
    keep = (offset >= -lower) & (offset <= upper) & (target >= 0) & (target < NBLK)
    return jnp.where(keep, target, -1).astype(jnp.int32)


def block_scale(stream_key, extent, cuts, low, largest):
    loudness, own = 1.0, jax.random.fold_in(stream_key, 6)
    for dim, parts in cuts:
        draws = jnp.exp(jax.random.uniform(jax.random.fold_in(own, dim), (parts,), jnp.float32, low / len(cuts), largest / len(cuts)))
        loudness = loudness * jnp.repeat(draws, extent[dim] // parts).reshape([-1 if axis == dim else 1 for axis in range(len(extent))])
    return loudness


def normal_values(rng, extent, scale, limit, cuts=(), kind=jnp.bfloat16):
    loudness = block_scale(rng, extent, cuts, -0.22, 0.18) if cuts else 1.0
    entries = jax.random.normal(rng, extent, jnp.float32) * scale * loudness
    return jnp.minimum(jnp.maximum(entries, -limit), limit).astype(kind)


def setup_inputs(seed: int = 0) -> dict:
    key_of = jax.random.split(jax.random.key(seed), 7)
    return {
        "query": draw_query(jax.random.fold_in(key_of[6], 71), 0),
        "keys": draw_keys(jax.random.fold_in(key_of[6], 71), 0),
        "values": normal_values(key_of[2], (FRAMES, WIDTH), 1.0, 6.0, ((0, 256),)),
        "grad_out": draw_grad_out(jax.random.fold_in(key_of[6], 71), 0),
        "band": draw_band(jax.random.fold_in(key_of[6], 71), 0),
        "prefix_len": jax.random.randint(key_of[5], (1,), PRE // 2, PRE + 1).astype(jnp.int32),
    }


def allowed_mask(band_rows, device, prefix_len, rows, block):
    per = rows // block
    kblock = (device - 1) * per + jnp.arange(3 * per, dtype=jnp.int32)
    match = jnp.any(band_rows[:, :, None] == kblock[None, None, :], axis=1) & (kblock >= 0)[None, :]
    grid = jnp.repeat(jnp.repeat(match, block, axis=0), block, axis=1)
    frame = (device - 1) * rows + jnp.arange(3 * rows, dtype=jnp.int32)
    grid = grid & (frame >= prefix_len[0])[None, :]
    prompt = jnp.arange(PRE, dtype=jnp.int32) < prefix_len[0]
    prompt = jnp.broadcast_to(prompt[None, :], (rows, PRE))
    return jnp.concatenate([grid, prompt], axis=1)


def attend_heads(query, cand_k, cand_v, grad_out, allowed):
    scale = HEAD ** -0.5
    qf = query.astype(jnp.float32).reshape(query.shape[0], HEADS, HEAD)
    gf = grad_out.astype(jnp.float32).reshape(query.shape[0], HEADS, HEAD)
    kf = cand_k.astype(jnp.float32).reshape(cand_k.shape[0], HEADS, HEAD)
    vf = cand_v.astype(jnp.float32).reshape(cand_v.shape[0], HEADS, HEAD)
    scores = jnp.einsum('qhd,khd->hqk', qf, kf) * scale
    scores = jnp.where(allowed[None], scores, -jnp.inf)
    top = jnp.max(scores, axis=-1, keepdims=True)
    expo = jnp.exp(scores - top)
    probs = expo / jnp.sum(expo, axis=-1, keepdims=True)
    probs_b = probs.astype(jnp.bfloat16).astype(jnp.float32)
    attended = jnp.einsum('hqk,khd->qhd', probs_b, vf).astype(jnp.bfloat16)
    dprobs = jnp.einsum('qhd,khd->hqk', gf, vf)
    delta = jnp.sum(probs * dprobs, axis=-1, keepdims=True)
    dscores = (probs * (dprobs - delta)).astype(jnp.bfloat16).astype(jnp.float32)
    grad_query = (jnp.einsum('hqk,khd->qhd', dscores, kf) * scale).astype(jnp.bfloat16)
    grad_keys = jnp.einsum('hqk,qhd->khd', dscores, qf) * scale
    grad_values = jnp.einsum('hqk,qhd->khd', probs_b, gf)
    rows = query.shape[0]
    width = HEADS * HEAD
    return (attended.reshape(rows, width), grad_query.reshape(rows, width),
            grad_keys.reshape(cand_k.shape[0], width), grad_values.reshape(cand_k.shape[0], width))


def reference(query, keys, values, grad_out, band, prefix_len):
    rows = F_DEV
    count = N_OUTER * N_INNER
    per = rows // BLK
    width = HEADS * HEAD
    zeros = jnp.zeros((rows, width), jnp.bfloat16)
    key_pad = jnp.concatenate([zeros, keys, zeros], axis=0)
    value_pad = jnp.concatenate([zeros, values, zeros], axis=0)
    prompt_k = keys[:PRE]
    prompt_v = values[:PRE]

    def step(carry, device):
        carry_k, carry_v, sum_k, sum_v = carry
        start = (device * rows).astype(jnp.int32)
        qrows = lax.dynamic_slice_in_dim(query, start, rows, 0)
        grows = lax.dynamic_slice_in_dim(grad_out, start, rows, 0)
        cand_k = jnp.concatenate([lax.dynamic_slice_in_dim(key_pad, start, 3 * rows, 0), prompt_k], axis=0)
        cand_v = jnp.concatenate([lax.dynamic_slice_in_dim(value_pad, start, 3 * rows, 0), prompt_v], axis=0)
        band_rows = lax.dynamic_slice_in_dim(band, (device * per).astype(jnp.int32), per, 0)
        allowed = allowed_mask(band_rows, device, prefix_len, rows, BLK)
        attended, grad_query, part_k, part_v = attend_heads(qrows, cand_k, cand_v, grows, allowed)
        band_k = part_k[:3 * rows].astype(jnp.bfloat16)
        band_v = part_v[:3 * rows].astype(jnp.bfloat16)
        own_k = band_k[rows:2 * rows].astype(jnp.float32) + carry_k
        own_v = band_v[rows:2 * rows].astype(jnp.float32) + carry_v
        new_carry = (band_k[2 * rows:].astype(jnp.float32), band_v[2 * rows:].astype(jnp.float32),
                     sum_k + part_k[3 * rows:], sum_v + part_v[3 * rows:])
        return new_carry, (attended, grad_query, own_k, own_v, band_k[:rows], band_v[:rows])

    init = (jnp.zeros((rows, width), jnp.float32), jnp.zeros((rows, width), jnp.float32),
            jnp.zeros((PRE, width), jnp.float32), jnp.zeros((PRE, width), jnp.float32))
    devices = jnp.arange(count, dtype=jnp.int32)
    final, stacked = lax.scan(step, init, devices)
    sum_k, sum_v = final[2], final[3]
    attended, grad_query, own_k, own_v, back_k, back_v = stacked
    tail = jnp.zeros((1, rows, width), jnp.bfloat16)
    total_k = own_k + jnp.concatenate([back_k[1:], tail], axis=0).astype(jnp.float32)
    total_v = own_v + jnp.concatenate([back_v[1:], tail], axis=0).astype(jnp.float32)
    total_k = total_k.reshape(count * rows, width)
    total_v = total_v.reshape(count * rows, width)
    total_k = total_k.at[:PRE].add(sum_k)
    total_v = total_v.at[:PRE].add(sum_v)
    return (attended.reshape(count * rows, width), grad_query.reshape(count * rows, width),
            total_k.astype(jnp.bfloat16), total_v.astype(jnp.bfloat16))
```

```python
import functools

import jax
import jax.numpy as jnp
from jax import lax
from jax.experimental import pallas as pl
from jax.experimental.pallas import tpu as pltpu
from jax.sharding import PartitionSpec as P

F32 = jnp.float32
BF = jnp.bfloat16
MESH = pl.DeviceIdType.MESH
BLK = 256
ROWS = 512
WIDTH = 512
PAIR = 128
PAIRS = 4
HEAD = 64
SLOTS = 5
TILES = 7
KEYS = TILES * BLK
CAND = 2048
SCALE = HEAD ** -0.5
TO_EXP2 = SCALE * 1.4426950408889634
OFF = -1e30
PLANE = 16
PIECE = 32


def dot_last(a, b):
    return lax.dot_general(a, b, (((1,), (1,)), ((), ())), preferred_element_type=F32)


def dot(a, b):
    return lax.dot_general(a, b, (((1,), (0,)), ((), ())), preferred_element_type=F32)


def tile_rows(qb, s):
    low = (qb + s) * BLK if s < SLOTS else 3 * ROWS + (s - SLOTS) * BLK
    return slice(low, low + BLK)


def fill_bias(band, plen, bias, device):
    row = lax.broadcasted_iota(jnp.int32, (BLK, PAIR), 0)
    for qb in range(2):
        for s in range(SLOTS):
            block = 2 * device + qb - 2 + s
            ok = (block * BLK + row >= plen[0]) & (band[qb, s] >= 0)
            bias[qb, s * BLK : (s + 1) * BLK, :] = jnp.where(ok, 0.0, OFF)
        for s in range(2):
            low = (SLOTS + s) * BLK
            bias[qb, low : low + BLK, :] = jnp.where(row + s * BLK < plen[0], 0.0, OFF)


def attend_pair(p, q, g, kv, bias, kt, vt, gt, x, e, dk, dv, att_t, dq_t, att, dq):
    cols = pl.ds(pl.multiple_of(p * PAIR, PAIR), PAIR)
    lane = lax.broadcasted_iota(jnp.int32, (BLK, PAIR), 1)
    kt[...] = kv[0, :, cols].T
    vt[...] = kv[1, :, cols].T
    gt[...] = g[:, cols].T
    dk[...] = jnp.zeros_like(dk)
    dv[...] = jnp.zeros_like(dv)
    for qb in range(2):
        mine = slice(qb * BLK, (qb + 1) * BLK)
        for h in range(2):
            half = (lane < HEAD) if h == 0 else (lane >= HEAD)
            heads = slice(h * HEAD, (h + 1) * HEAD)
            qz = jnp.where(half, q[mine, cols], jnp.zeros((), BF))
            top = jnp.full((8, BLK), OFF, F32)
            for s in range(TILES):
                t = dot_last(kv[0, tile_rows(qb, s), cols], qz) * TO_EXP2
                b = bias[qb, s * BLK : (s + 1) * BLK, :]
                t = t + jnp.concatenate([b, b], axis=1)
                x[s * BLK : (s + 1) * BLK, :] = t
                top = jnp.maximum(top, jnp.max(t.reshape(BLK // 8, 8, BLK), axis=0))
            top = jnp.max(top, axis=0, keepdims=True)
            total = jnp.zeros((8, BLK), F32)
            a = jnp.zeros((HEAD, BLK), F32)
            for s in range(TILES):
                expo = jnp.exp2(x[s * BLK : (s + 1) * BLK, :] - top)
                total = total + jnp.sum(expo.reshape(BLK // 8, 8, BLK), axis=0)
                eb = expo.astype(BF)
                e[s * BLK : (s + 1) * BLK, :] = eb
                a = a + dot(vt[heads, tile_rows(qb, s)], eb)
            r = 1.0 / jnp.sum(total, axis=0, keepdims=True)
            a = a * r
            att_t[heads, :] = a
            r_col = jnp.broadcast_to(r, (PAIR, BLK)).T
            gz = jnp.where(half, g[mine, cols].astype(F32) * r_col, 0.0).astype(BF)
            g_row = (gt[heads, mine].astype(F32) * r).astype(BF).astype(F32)
            delta = jnp.sum(g_row * a, axis=0, keepdims=True)
            d = jnp.zeros((HEAD, BLK), F32)
            for s in range(TILES):
                rows = tile_rows(qb, s)
                eb = e[s * BLK : (s + 1) * BLK, :]
                dp = dot_last(kv[1, rows, cols], gz) - delta
                ds = (eb.astype(F32) * dp).astype(BF)
                dv[rows, :] += dot(eb, gz)
                dk[rows, :] += dot(ds, qz)
                d = d + dot(kt[heads, rows], ds)
            dq_t[heads, :] = d * SCALE
        att[mine, cols] = att_t[...].T.astype(BF)
        dq[mine, cols] = dq_t[...].T.astype(BF)


def wait_bytes(ref, sem):
    pltpu.make_async_copy(ref, ref, sem).wait()


def kernel(
    band, plen, q, k, v, g, att, dq, out_k, out_v,
    kv, bias, kt, vt, gt, x, e, dk, dv, att_t, dq_t,
    own, ys, yr, xs, xr, ps, pr, rb, rc, pz, rz, pf, rf,
    local_sem, hx_s, hx_r, hy_s, hy_r, b1_s, b1_r, b2_s, b2_r, b3_s, b3_r, b4_s, b4_r,
    y_s, y_r, x_s, x_r, r1_s, r1_r, r2_s, r2_r, r3_s, r3_r, r4_s, r4_r,
):
    outer = lax.axis_index("outer")
    inner = lax.axis_index("inner")
    device = outer * 8 + inner
    z = outer // 4
    x_lo = (outer // 2) % 2
    core = outer % 2
    spot = x_lo * 8 + inner
    odd = inner % 2
    partner = (outer, inner + 1 - 2 * odd)
    ahead = lax.rem(device + 2 - 4 * odd + 256, 256)
    behind = lax.rem(device - 2 + 4 * odd + 256, 256)
    ahead = (ahead // 8, ahead % 8)
    behind = (behind // 8, behind % 8)
    other_core = (outer + 1 - 2 * core, inner)
    root = (0, 0)
    first = device == 0
    bottom = z == 0

    def in_plane(level, at, which):
        return ((level * 2 + at // 8) * 2 + which, at % 8)

    def in_column(level):
        return ((level * 2 + x_lo) * 2 + core, inner)

    def plane_peer(n):
        return lax.rem(spot + 1 + n, PLANE)

    def root_peer(n):
        return in_plane(0, n % PLANE, n // PLANE)

    mine_in = [
        pltpu.make_async_copy(k, kv.at[0, pl.ds(ROWS, ROWS)], local_sem.at[0]),
        pltpu.make_async_copy(v, kv.at[1, pl.ds(ROWS, ROWS)], local_sem.at[1]),
    ]
    for c in mine_in:
        c.start()

    barrier = pltpu.get_barrier_semaphore()

    def hello(target):
        pl.semaphore_signal(barrier, inc=1, device_id=target, device_id_type=MESH)

    for target in (partner, ahead, behind, other_core):
        hello(target)

    @pl.loop(0, PLANE - 1)
    def _(n):
        hello(in_plane(z, plane_peer(n), core))

    @pl.when(bottom)
    def _():
        @pl.loop(1, 8)
        def _(n):
            hello(in_column(n))

    @pl.when(jnp.logical_not(bottom))
    def _():
        hello(in_column(0))

    @pl.when(first)
    def _():
        @pl.loop(1, 2 * PLANE)
        def _(n):
            hello(root_peer(n))

    @pl.when(jnp.logical_and(bottom, jnp.logical_not(first)))
    def _():
        hello(root)

    for c in mine_in:
        c.wait()
    greeted = 4 + PLANE - 1 + jnp.where(bottom, 7, 1)
    greeted = greeted + jnp.where(first, 2 * PLANE - 1, jnp.where(bottom, 1, 0))
    pl.semaphore_wait(barrier, greeted)

    def send(src, dst, s_sem, r_sem, target):
        return pltpu.make_async_remote_copy(
            src_ref=src, dst_ref=dst, send_sem=s_sem, recv_sem=r_sem,
            device_id=target, device_id_type=MESH,
        )

    far = pl.multiple_of(odd * 1024, ROWS)
    near = pl.multiple_of((1 - odd) * 1024, ROWS)

    def columns(c):
        return pl.ds(pl.multiple_of(c * PAIR, PAIR), PAIR)

    def halo_x(c):
        return send(
            kv.at[:, pl.ds(ROWS, ROWS), columns(c)], kv.at[:, pl.ds(far, ROWS), columns(c)],
            hx_s.at[c], hx_r.at[c], partner,
        )

    def halo_y(c):
        return send(
            kv.at[:, pl.ds(near, ROWS), columns(c)], kv.at[:, pl.ds(far, ROWS), columns(c)],
            hy_s.at[c], hy_r.at[c], ahead,
        )

    def piece(at):
        return kv.at[core, pl.ds(pl.multiple_of(3 * ROWS + at * PIECE, PIECE), PIECE)]

    @pl.when(first)
    def _():
        @pl.loop(1, 2 * PLANE)
        def _(n):
            at = n % PLANE
            which = n // PLANE
            send(
                kv.at[which, pl.ds(pl.multiple_of(ROWS + at * PIECE, PIECE), PIECE)],
                kv.at[which, pl.ds(pl.multiple_of(3 * ROWS + at * PIECE, PIECE), PIECE)],
                b1_s, b1_r, root_peer(n),
            ).start()

        own_piece = pltpu.make_async_copy(
            kv.at[0, pl.ds(ROWS, PIECE)], kv.at[0, pl.ds(3 * ROWS, PIECE)], local_sem.at[0]
        )
        own_piece.start()
        own_piece.wait()

    @pl.loop(0, PAIRS)
    def _(c):
        halo_x(c).start()

    fill_bias(band, plen, bias, device)

    @pl.when(jnp.logical_and(bottom, jnp.logical_not(first)))
    def _():
        wait_bytes(piece(spot), b1_r)

    @pl.when(bottom)
    def _():
        @pl.loop(1, 8)
        def _(n):
            send(piece(spot), piece(spot), b2_s, b2_r, in_column(n)).start()

    @pl.when(jnp.logical_not(bottom))
    def _():
        wait_bytes(piece(spot), b2_r)

    @pl.loop(0, PLANE - 1)
    def _(n):
        send(piece(spot), piece(spot), b3_s, b3_r, in_plane(z, plane_peer(n), core)).start()

    @pl.loop(0, 2)
    def _(c):
        halo_x(c).wait_recv()
        halo_y(c).start()

    most = (PLANE - 1) * PIECE
    wait_bytes(kv.at[0, pl.ds(0, most)], b3_r)
    whole = kv.at[core, pl.ds(3 * ROWS, ROWS)]
    prompt = send(whole, whole, b4_s, b4_r, other_core)
    prompt.start()

    @pl.loop(2, PAIRS)
    def _(c):
        halo_x(c).wait_recv()
        halo_y(c).start()

    prompt.wait()

    def y_back(c):
        return send(ys.at[:, :, columns(c)], yr.at[:, :, columns(c)], y_s.at[c], y_r.at[c], behind)

    def x_back(c):
        return send(xs.at[:, :, columns(c)], xr.at[:, :, columns(c)], x_s.at[c], x_r.at[c], partner)

    def swap(c):
        return send(ps.at[1 - core, :, columns(c)], pr.at[:, columns(c)], r1_s.at[c], r1_r.at[c], other_core)

    def scatter(c, n):
        to = plane_peer(n)
        return send(
            rb.at[pl.ds(pl.multiple_of(to * PIECE, PIECE), PIECE), columns(c)],
            rc.at[spot, :, columns(c)], r2_s.at[c], r2_r.at[c], in_plane(z, to, core),
        )

    def sink(c):
        return send(pz.at[:, columns(c)], rz.at[z, :, columns(c)], r3_s.at[c], r3_r.at[c], in_column(0))

    def place():
        return pl.ds(pl.multiple_of(core * ROWS + spot * PIECE, PIECE), PIECE)

    def collect(c):
        return send(pf.at[:, columns(c)], rf.at[place(), columns(c)], r4_s.at[c], r4_r.at[c], root)

    @pl.loop(0, PAIRS + 4)
    def _(t):
        @pl.when(t < PAIRS)
        def _():
            halo_y(t).wait_recv()
            attend_pair(t, q, g, kv, bias, kt, vt, gt, x, e, dk, dv, att_t, dq_t, att, dq)
            cols = columns(t)
            for n, grad, scale in ((0, dk, SCALE), (1, dv, 1.0)):
                ys[n, :, cols] = (grad[pl.ds(far, ROWS), :] * scale).astype(BF)
                xs[n, :, cols] = (grad[pl.ds(near, ROWS), :] * scale).astype(BF)
                own[n, :, cols] = grad[pl.ds(ROWS, ROWS), :] * scale
                ps[n, :, cols] = (grad[pl.ds(3 * ROWS, ROWS), :] * scale).astype(BF)
            y_back(t).start()
            swap(t).start()

        @pl.when(jnp.logical_and(t >= 1, t < PAIRS + 1))
        def _():
            c = t - 1
            cols = columns(c)
            swap(c).wait_recv()
            rb[:, cols] = (ps[core, :, cols].astype(F32) + pr[:, cols].astype(F32)).astype(BF)

            @pl.loop(0, PLANE - 1)
            def _(n):
                scatter(c, n).start()

            y_back(c).wait_recv()
            for n in range(2):
                xs[n, :, cols] = (xs[n, :, cols].astype(F32) + yr[n, :, cols].astype(F32)).astype(BF)
            x_back(c).start()

        @pl.when(jnp.logical_and(t >= 2, t < PAIRS + 2))
        def _():
            c = t - 2
            cols = columns(c)
            wait_bytes(rc.at[pl.ds(0, PLANE - 1), :, columns(0)], r2_r.at[c])
            rc[spot, :, cols] = rb[pl.ds(pl.multiple_of(spot * PIECE, PIECE), PIECE), cols]
            part = rc[0, :, cols].astype(F32)
            for n in range(1, PLANE):
                part = part + rc[n, :, cols].astype(F32)
            pz[:, cols] = part

            @pl.when(jnp.logical_not(bottom))
            def _():
                sink(c).start()

            x_back(c).wait_recv()
            for n in range(2):
                own[n, :, cols] += xr[n, :, cols].astype(F32)

        @pl.when(jnp.logical_and(bottom, jnp.logical_and(t >= 3, t < PAIRS + 3)))
        def _():
            c = t - 3
            cols = columns(c)
            wait_bytes(rz.at[pl.ds(1, 7), :, columns(0)], r3_r.at[c])
            part = pz[:, cols]
            for n in range(1, 8):
                part = part + rz[n, :, cols]
            pf[:, cols] = part

            @pl.when(first)
            def _():
                rf[pl.ds(0, PIECE), cols] = part

            @pl.when(jnp.logical_not(first))
            def _():
                collect(c).start()

        @pl.when(jnp.logical_and(first, t >= 4))
        def _():
            c = t - 4
            cols = columns(c)
            wait_bytes(rf.at[pl.ds(0, (2 * PLANE - 1) * PIECE), columns(0)], r4_r.at[c])
            for n in range(2):
                own[n, :, cols] += rf[pl.ds(n * ROWS, ROWS), cols]

    out_k[...] = own[0].astype(BF)
    out_v[...] = own[1].astype(BF)

    @pl.loop(0, PAIRS)
    def _(c):
        halo_x(c).wait_send()
        halo_y(c).wait_send()
        y_back(c).wait_send()
        x_back(c).wait_send()
        swap(c).wait_send()
        wait_bytes(rc.at[pl.ds(0, PLANE - 1), :, columns(0)], r2_s.at[c])

        @pl.when(jnp.logical_not(bottom))
        def _():
            sink(c).wait_send()

        @pl.when(jnp.logical_and(bottom, jnp.logical_not(first)))
        def _():
            collect(c).wait_send()

    wait_bytes(kv.at[0, pl.ds(0, most)], b3_s)

    @pl.when(bottom)
    def _():
        wait_bytes(kv.at[0, pl.ds(0, 7 * PIECE)], b2_s)

    @pl.when(first)
    def _():
        wait_bytes(kv.at[0, pl.ds(0, (2 * PLANE - 1) * PIECE)], b1_s)


def on_device(query, keys, values, grad_out, band, prefix_len):
    vmem = pl.BlockSpec(memory_space=pltpu.VMEM)
    smem = pl.BlockSpec(memory_space=pltpu.SMEM)
    hbm = pl.BlockSpec(memory_space=pl.ANY)
    dma = pltpu.SemaphoreType.DMA
    return pl.pallas_call(
        kernel,
        out_shape=[jax.ShapeDtypeStruct((ROWS, WIDTH), BF)] * 4,
        in_specs=[smem, smem, vmem, hbm, hbm, vmem],
        out_specs=[vmem] * 4,
        scratch_shapes=[
            pltpu.VMEM((2, CAND, WIDTH), BF),
            pltpu.VMEM((2, KEYS, PAIR), F32),
            pltpu.VMEM((PAIR, CAND), BF),
            pltpu.VMEM((PAIR, CAND), BF),
            pltpu.VMEM((PAIR, ROWS), BF),
            pltpu.VMEM((KEYS, BLK), F32),
            pltpu.VMEM((KEYS, BLK), BF),
            pltpu.VMEM((CAND, PAIR), F32),
            pltpu.VMEM((CAND, PAIR), F32),
            pltpu.VMEM((PAIR, BLK), F32),
            pltpu.VMEM((PAIR, BLK), F32),
            pltpu.VMEM((2, ROWS, WIDTH), F32),
            pltpu.VMEM((2, ROWS, WIDTH), BF),
            pltpu.VMEM((2, ROWS, WIDTH), BF),
            pltpu.VMEM((2, ROWS, WIDTH), BF),
            pltpu.VMEM((2, ROWS, WIDTH), BF),
            pltpu.VMEM((2, ROWS, WIDTH), BF),
            pltpu.VMEM((ROWS, WIDTH), BF),
            pltpu.VMEM((ROWS, WIDTH), BF),
            pltpu.VMEM((PLANE, PIECE, WIDTH), BF),
            pltpu.VMEM((PIECE, WIDTH), F32),
            pltpu.VMEM((8, PIECE, WIDTH), F32),
            pltpu.VMEM((PIECE, WIDTH), F32),
            pltpu.VMEM((2 * ROWS, WIDTH), F32),
            dma((2,)),
            dma((PAIRS,)), dma((PAIRS,)), dma((PAIRS,)), dma((PAIRS,)),
            dma, dma, dma, dma, dma, dma, dma, dma,
            dma((PAIRS,)), dma((PAIRS,)), dma((PAIRS,)), dma((PAIRS,)),
            dma((PAIRS,)), dma((PAIRS,)), dma((PAIRS,)), dma((PAIRS,)),
            dma((PAIRS,)), dma((PAIRS,)), dma((PAIRS,)), dma((PAIRS,)),
        ],
        compiler_params=pltpu.CompilerParams(
            collective_id=0, has_side_effects=True, vmem_limit_bytes=58 * 2**20
        ),
        name="banded",
    )(band, prefix_len, query, keys, values, grad_out)


def solution(mesh):
    rows = P(("outer", "inner"), None)
    return jax.shard_map(
        on_device,
        mesh=mesh,
        in_specs=(rows, rows, rows, rows, rows, P()),
        out_specs=(rows, rows, rows, rows),
        check_vma=False,
    )
```

```python
import functools

import jax
import jax.numpy as jnp
from jax import lax
from jax.experimental import pallas as pl
from jax.experimental.pallas import tpu as pltpu
from jax.sharding import PartitionSpec as P

F32 = jnp.float32
BF = jnp.bfloat16
MESH = pl.DeviceIdType.MESH
BLK = 256
ROWS = 512
WIDTH = 512
PAIR = 128
PAIRS = 2
HEAD = 64
SLOTS = 5
TILES = 7
KEYS = TILES * BLK
CAND = 2560
PROMPT = 2048
MINE = 256
SCALE = HEAD ** -0.5
TO_EXP2 = SCALE * 1.4426950408889634
OFF = -1e30
PLANE = 8
PIECE = 64


def dot_last(a, b):
    return lax.dot_general(a, b, (((1,), (1,)), ((), ())), preferred_element_type=F32)


def dot(a, b):
    return lax.dot_general(a, b, (((1,), (0,)), ((), ())), preferred_element_type=F32)


def at_block(start):
    return pl.ds(pl.multiple_of(start, BLK), BLK)


def fill_bias(listed, plen, bias, base):
    row = lax.broadcasted_iota(jnp.int32, (BLK, PAIR), 0)
    for i in range(4):
        for s in range(SLOTS):
            ok = (base + i - 2 + s) * BLK + row >= plen[0]
            n = (i % 2) * SLOTS + s
            bias[i, s * BLK : (s + 1) * BLK, :] = jnp.where(ok, listed[i // 2, n : n + 1, :], OFF)
        for s in range(2):
            low = (SLOTS + s) * BLK
            bias[i, low : low + BLK, :] = jnp.where(row + s * BLK < plen[0], 0.0, OFF)


def attend(p, u, kv, qg, bias, kt, vt, gt, x, e, dk, dv, att_t, dq_t, result):
    cols = pl.ds(pl.multiple_of(p * PAIR, PAIR), PAIR)
    lane = lax.broadcasted_iota(jnp.int32, (BLK, PAIR), 1)
    combos = [(qb, h) for qb in range(2) for h in range(2)]

    def half(h):
        return (lane < HEAD) if h == 0 else (lane >= HEAD)

    def heads(h):
        return slice(h * HEAD, (h + 1) * HEAD)

    def mine(qb):
        return at_block(u * ROWS + qb * BLK)

    def keys_of(qb, s):
        return at_block(u * ROWS + (qb + s) * BLK) if s < SLOTS else at_block(PROMPT + (s - SLOTS) * BLK)

    qz = [jnp.where(half(h), qg[0, mine(qb), cols], jnp.zeros((), BF)) for qb, h in combos]

    def score(n):
        qb, h = combos[n]
        top = jnp.full((8, BLK), OFF, F32)
        for s in range(TILES):
            t = dot_last(kv[0, keys_of(qb, s), cols], qz[n]) * TO_EXP2
            b = bias[2 * u + qb, s * BLK : (s + 1) * BLK, :]
            t = t + jnp.concatenate([b, b], axis=1)
            x[n, s * BLK : (s + 1) * BLK, :] = t
            top = jnp.maximum(top, jnp.max(t.reshape(BLK // 8, 8, BLK), axis=0))
        return jnp.max(top, axis=0, keepdims=True)

    def weigh(n, top):
        qb, h = combos[n]
        total = jnp.zeros((8, BLK), F32)
        a = jnp.zeros((HEAD, BLK), F32)
        for s in range(TILES):
            expo = jnp.exp2(x[n, s * BLK : (s + 1) * BLK, :] - top)
            total = total + jnp.sum(expo.reshape(BLK // 8, 8, BLK), axis=0)
            eb = expo.astype(BF)
            e[n, s * BLK : (s + 1) * BLK, :] = eb
            a = a + dot(vt[heads(h), keys_of(qb, s)], eb)
        r = 1.0 / jnp.sum(total, axis=0, keepdims=True)
        a = a * r
        att_t[qb, heads(h), :] = a
        r_col = jnp.broadcast_to(r, (PAIR, BLK)).T
        gz = jnp.where(half(h), qg[1, mine(qb), cols].astype(F32) * r_col, 0.0).astype(BF)
        g_row = (gt[heads(h), mine(qb)].astype(F32) * r).astype(BF).astype(F32)
        return gz, jnp.sum(g_row * a, axis=0, keepdims=True)

    def differentiate(n, gz, delta):
        qb, h = combos[n]
        d = jnp.zeros((HEAD, BLK), F32)
        band_rows = pl.ds(pl.multiple_of(u * ROWS + qb * BLK, BLK), SLOTS * BLK)
        for low, count, rows in ((0, SLOTS * BLK, band_rows), (SLOTS * BLK, 2 * BLK, pl.ds(PROMPT, 2 * BLK))):
            eb = e[n, low : low + count, :]
            dp = dot_last(kv[1, rows, cols], gz) - delta
            ds = (eb.astype(F32) * dp).astype(BF)
            dv[rows, :] += dot(eb, gz)
            dk[rows, :] += dot(ds, qz[n])
            d = d + dot(kt[heads(h), rows], ds)
        dq_t[qb, heads(h), :] = d * SCALE

    tops = [score(0)]
    grads = []
    for n in range(4):
        if n < 3:
            tops.append(score(n + 1))
        grads.append(weigh(n, tops[n]))
        if n >= 1:
            differentiate(n - 1, *grads[n - 1])
    differentiate(3, *grads[3])
    for qb in range(2):
        result[0, mine(qb), cols] = att_t[qb].T.astype(BF)
        result[1, mine(qb), cols] = dq_t[qb].T.astype(BF)


def wait_bytes(ref, sem):
    pltpu.make_async_copy(ref, ref, sem).wait()


def kernel(
    band, plen, q, k, v, g, att, dq, out_k, out_v,
    kv, qg, listed, bias, kt, vt, gt, x, e, dk, dv, att_t, dq_t, result,
    own, near_s, near_r, far_s, far_r, xo, xr, ps, pr, rb, ry, pz, rz, pf, rf,
    local_sem, l_s, l_r, x_s, x_r, e_s, e_r, f_s, f_r,
    b1_s, b1_r, b2_s, b2_r, b3_s, b3_r, b4_s, b4_r,
    n_s, n_r, w_s, w_r, o_s, o_r, r1_s, r1_r, r2_s, r2_r, r3_s, r3_r, r4_s, r4_r,
):
    outer = lax.axis_index("outer")
    inner = lax.axis_index("inner")
    device = outer * 8 + inner
    z = outer // 4
    x_lo = (outer // 2) % 2
    core = outer % 2
    side = inner % 2
    spot = (inner // 2) * 2 + x_lo
    partner = (outer, inner + 1 - 2 * side)
    up = lax.rem(device + 2, 256)
    down = lax.rem(device + 254, 256)
    near = jnp.where(side == 0, down, up)
    far = jnp.where(side == 0, up, down)
    near = (near // 8, near % 8)
    far = (far // 8, far % 8)
    other_core = (outer + 1 - 2 * core, inner)
    root = (0, 0)
    first = device == 0
    bottom = z == 0

    def in_plane(level, at, part, which):
        return ((level * 2 + at % 2) * 2 + which, (at // 2) * 2 + part)

    def in_column(level):
        return ((level * 2 + x_lo) * 2 + core, inner)

    def peer(n):
        return lax.rem(spot + n, PLANE)

    def lanes(part):
        return pl.ds(pl.multiple_of(part * MINE, MINE), MINE)

    def columns(c):
        return pl.ds(pl.multiple_of(c * PAIR, PAIR), PAIR)

    def run(part):
        return pl.ds(pl.multiple_of(part * ROWS, ROWS), ROWS)

    own_rows = run(1 + side)
    near_rows = pl.ds(pl.multiple_of((1 - side) * 3 * ROWS, ROWS), ROWS)
    far_rows = pl.ds(pl.multiple_of(side * 3 * ROWS, ROWS), ROWS)
    held = [(k, kv.at[0], own_rows), (v, kv.at[1], own_rows), (q, qg.at[0], run(side)), (g, qg.at[1], run(side))]
    mine_in = [
        pltpu.make_async_copy(src.at[:, lanes(side)], dst.at[rows], local_sem.at[n])
        for n, (src, dst, rows) in enumerate(held)
    ]
    for c in mine_in:
        c.start()
    for qb in range(2):
        for s in range(SLOTS):
            n = qb * SLOTS + s
            listed[side, n : n + 1, :] = jnp.full((1, PAIR), jnp.where(band[qb, s] >= 0, 0.0, OFF), F32)
    for n in range(2 * SLOTS, 16):
        listed[side, n : n + 1, :] = jnp.zeros((1, PAIR), F32)

    barrier = pltpu.get_barrier_semaphore()

    def hello(target):
        pl.semaphore_signal(barrier, inc=1, device_id=target, device_id_type=MESH)

    for target in (partner, near, far, other_core):
        hello(target)
    for n in range(1, PLANE):
        hello(in_plane(z, peer(n), side, core))

    @pl.when(bottom)
    def _():
        @pl.loop(1, 8)
        def _(n):
            hello(in_column(n))

    @pl.when(jnp.logical_not(bottom))
    def _():
        hello(in_column(0))

    def root_peer(n):
        return in_plane(0, n % PLANE, (n // PLANE) % 2, n // (2 * PLANE))

    @pl.when(first)
    def _():
        @pl.loop(1, 4 * PLANE)
        def _(n):
            hello(root_peer(n))

    @pl.when(jnp.logical_and(bottom, jnp.logical_not(first)))
    def _():
        hello(root)

    greeted = 4 + PLANE - 1 + jnp.where(bottom, 7, 1)
    greeted = greeted + jnp.where(first, 4 * PLANE - 1, jnp.where(bottom, 1, 0))
    for c in mine_in:
        c.wait()
    pl.semaphore_wait(barrier, greeted)

    def send(src, dst, s_sem, r_sem, target):
        return pltpu.make_async_remote_copy(
            src_ref=src, dst_ref=dst, send_sem=s_sem, recv_sem=r_sem,
            device_id=target, device_id_type=MESH,
        )

    def cross(c):
        lane = pl.ds(pl.multiple_of((1 - side) * MINE + c * PAIR, PAIR), PAIR)
        return [
            send(src.at[:, lane], dst.at[rows, columns(c)], x_s.at[4 * c + n], x_r.at[4 * c + n], partner)
            for n, (src, dst, rows) in enumerate(held)
        ]

    def to_near(c):
        return send(
            kv.at[:, own_rows, columns(c)], kv.at[:, near_rows, columns(c)], e_s.at[c], e_r.at[c], near
        )

    def to_far(c):
        return send(
            kv.at[:, run(2 - side), columns(c)], kv.at[:, far_rows, columns(c)], f_s.at[c], f_r.at[c], far
        )

    def strip(at):
        return pl.ds(pl.multiple_of(at * PIECE, PIECE), PIECE)

    def piece(which, at):
        return kv.at[which, pl.ds(pl.multiple_of(PROMPT + at * PIECE, PIECE), PIECE)]

    @pl.when(first)
    def _():
        for which, src, low in ((0, k, 1), (1, v, 0)):

            @pl.loop(low, 2 * PLANE)
            def _(n):
                at = n % PLANE
                send(
                    src.at[strip(at), lanes(n // PLANE)], piece(which, at), b1_s, b1_r,
                    root_peer(n + which * 2 * PLANE),
                ).start()

        own_piece = pltpu.make_async_copy(k.at[strip(0), lanes(0)], piece(0, 0), local_sem.at[0])
        own_piece.start()
        own_piece.wait()

    note = send(listed.at[side], listed.at[side], l_s, l_r, partner)
    note.start()
    for c in cross(0):
        c.start()
    to_near(0).start()

    @pl.when(jnp.logical_and(bottom, jnp.logical_not(first)))
    def _():
        wait_bytes(piece(core, spot), b1_r)

    @pl.when(bottom)
    def _():
        @pl.loop(1, 8)
        def _(n):
            send(piece(core, spot), piece(core, spot), b2_s, b2_r, in_column(n)).start()

    note.wait()
    fill_bias(listed, plen, bias, 2 * (device - side))

    @pl.when(jnp.logical_not(bottom))
    def _():
        wait_bytes(piece(core, spot), b2_r)

    for n in range(1, PLANE):
        send(piece(core, spot), piece(core, spot), b3_s, b3_r, in_plane(z, peer(n), side, core)).start()
    for c in cross(0):
        c.wait_recv()
    to_far(0).start()
    for c in cross(1):
        c.start()
    to_near(1).start()
    wait_bytes(kv.at[0, pl.ds(0, (PLANE - 1) * PIECE)], b3_r)
    whole = kv.at[core, pl.ds(PROMPT, ROWS)]
    prompt = send(whole, whole, b4_s, b4_r, other_core)
    prompt.start()
    prompt.wait()

    def near_back(c):
        return send(near_s.at[:, :, columns(c)], near_r.at[:, :, columns(c)], n_s.at[c], n_r.at[c], near)

    def far_back(c):
        return send(far_s.at[:, :, columns(c)], far_r.at[:, :, columns(c)], w_s.at[c], w_r.at[c], far)

    def x_back(c):
        return [
            send(result.at[:, run(1 - side), columns(c)], xr.at[0:2, :, columns(c)], o_s.at[2 * c], o_r.at[2 * c], partner),
            send(xo.at[:, :, columns(c)], xr.at[2:4, :, columns(c)], o_s.at[2 * c + 1], o_r.at[2 * c + 1], partner),
        ]

    def swap(c):
        return send(ps.at[1 - core, :, columns(c)], pr.at[:, columns(c)], r1_s.at[c], r1_r.at[c], other_core)

    def scatter(c, n):
        to = peer(n)
        return send(
            rb.at[strip(to), columns(c)], ry.at[spot, :, columns(c)], r2_s.at[c], r2_r.at[c],
            in_plane(z, to, side, core),
        )

    def sink(c):
        return send(pz.at[:, columns(c)], rz.at[z, :, columns(c)], r3_s.at[c], r3_r.at[c], in_column(0))

    def collect(c):
        place = pl.ds(pl.multiple_of(core * ROWS + spot * PIECE, PIECE), PIECE)
        lane = pl.ds(pl.multiple_of(side * MINE + c * PAIR, PAIR), PAIR)
        return send(pf.at[:, columns(c)], rf.at[place, lane], r4_s.at[c], r4_r.at[c], root)

    def hand_back(c):
        cols = columns(c)
        x_back(c)[0].start()
        for n, grad, scale in ((0, dk, SCALE), (1, dv, 1.0)):
            ps[n, :, cols] = (grad[pl.ds(PROMPT, ROWS), :] * scale).astype(BF)
        swap(c).start()
        for n, grad, scale in ((0, dk, SCALE), (1, dv, 1.0)):
            far_s[n, :, cols] = (grad[near_back_rows[1], :] * scale).astype(BF)
        far_back(c).start()
        near_back(c).wait_recv()
        for n, grad, scale in ((0, dk, SCALE), (1, dv, 1.0)):
            xo[n, :, cols] = (grad[run(2 - side), :] * scale + near_r[n, :, cols].astype(F32)).astype(BF)
        x_back(c)[1].start()
        for n, grad, scale in ((0, dk, SCALE), (1, dv, 1.0)):
            own[n, :, cols] = grad[own_rows, :] * scale

    near_back_rows = (far_rows, near_rows)

    def reduce_plane(c):
        cols = columns(c)
        swap(c).wait_recv()
        rb[:, cols] = (ps[core, :, cols].astype(F32) + pr[:, cols].astype(F32)).astype(BF)
        for n in range(1, PLANE):
            scatter(c, n).start()

    def reduce_column(c):
        cols = columns(c)
        wait_bytes(ry.at[pl.ds(0, PLANE - 1), :, columns(0)], r2_r.at[c])
        ry[spot, :, cols] = rb[strip(spot), cols]
        part = ry[0, :, cols].astype(F32)
        for n in range(1, PLANE):
            part = part + ry[n, :, cols].astype(F32)
        pz[:, cols] = part

        @pl.when(jnp.logical_not(bottom))
        def _():
            sink(c).start()

    def reduce_root(c):
        cols = columns(c)

        @pl.when(bottom)
        def _():
            wait_bytes(rz.at[pl.ds(1, 7), :, columns(0)], r3_r.at[c])
            part = pz[:, cols]
            for n in range(1, 8):
                part = part + rz[n, :, cols]
            pf[:, cols] = part

            @pl.when(first)
            def _():
                rf[pl.ds(0, PIECE), cols] = part

            @pl.when(jnp.logical_not(first))
            def _():
                collect(c).start()

    def settle(c):
        cols = columns(c)
        far_back(c).wait_recv()
        for n in range(2):
            own[n, :, cols] += far_r[n, :, cols].astype(F32)

    @pl.loop(0, 4)
    def _(t):
        p = t // 2
        late = t % 2

        @pl.when(late == 0)
        def _():
            to_near(p).wait_recv()
            dk[...] = jnp.zeros_like(dk)
            dv[...] = jnp.zeros_like(dv)

            to_far(p).wait_recv()
            cols = columns(p)
            kt[...] = kv[0, :, cols].T
            vt[...] = kv[1, :, cols].T
            gt[...] = qg[1, :, cols].T

        @pl.when(t == 1)
        def _():
            for c in cross(1):
                c.wait_recv()
            to_far(1).start()

        u = jnp.where(late == 0, side, 1 - side)
        attend(p, u, kv, qg, bias, kt, vt, gt, x, e, dk, dv, att_t, dq_t, result)

        @pl.when(late == 0)
        def _():
            cols = columns(p)
            for n, grad, scale in ((0, dk, SCALE), (1, dv, 1.0)):
                near_s[n, :, cols] = (grad[near_back_rows[0], :] * scale).astype(BF)
            near_back(p).start()

        @pl.when(t == 1)
        def _():
            hand_back(0)

        @pl.when(t == 2)
        def _():
            reduce_plane(0)

        @pl.when(t == 3)
        def _():
            hand_back(1)
            reduce_column(0)

    reduce_plane(1)
    reduce_root(0)
    settle(0)
    reduce_column(1)
    for n, ref in ((0, att), (1, dq)):
        ref[:, lanes(side)] = result[n, run(side), :]
    settle(1)
    reduce_root(1)
    for c in range(PAIRS):
        for copy in x_back(c):
            copy.wait_recv()

    @pl.when(first)
    def _():
        for c in range(PAIRS):
            wait_bytes(rf.at[pl.ds(0, (4 * PLANE - 1) * PIECE // 2), lanes(0)], r4_r.at[c])
        for n in range(2):
            own[n] += rf[pl.ds(n * ROWS, ROWS), lanes(0)]
            xr[2 + n] = (xr[2 + n].astype(F32) + rf[pl.ds(n * ROWS, ROWS), lanes(1)]).astype(BF)

    for n, ref in enumerate((att, dq, out_k, out_v)):
        ref[:, lanes(1 - side)] = xr[n]
    for n, ref in ((0, out_k), (1, out_v)):
        ref[:, lanes(side)] = own[n].astype(BF)

    for c in range(PAIRS):
        for copy in cross(c) + x_back(c):
            copy.wait_send()
        for copy in (to_near(c), to_far(c), near_back(c), far_back(c), swap(c)):
            copy.wait_send()
        wait_bytes(ry.at[pl.ds(0, PLANE - 1), :, columns(0)], r2_s.at[c])

        @pl.when(jnp.logical_not(bottom))
        def _(c=c):
            sink(c).wait_send()

        @pl.when(jnp.logical_and(bottom, jnp.logical_not(first)))
        def _(c=c):
            collect(c).wait_send()

    wait_bytes(kv.at[0, pl.ds(0, (PLANE - 1) * PIECE)], b3_s)

    @pl.when(bottom)
    def _():
        wait_bytes(kv.at[0, pl.ds(0, 7 * PIECE)], b2_s)

    @pl.when(first)
    def _():
        wait_bytes(kv.at[0, pl.ds(0, (4 * PLANE - 1) * PIECE)], b1_s)


def on_device(query, keys, values, grad_out, band, prefix_len):
    vmem = pl.BlockSpec(memory_space=pltpu.VMEM)
    smem = pl.BlockSpec(memory_space=pltpu.SMEM)
    hbm = pl.BlockSpec(memory_space=pl.ANY)
    dma = pltpu.SemaphoreType.DMA
    two = dma((PAIRS,))
    return pl.pallas_call(
        kernel,
        out_shape=[jax.ShapeDtypeStruct((ROWS, WIDTH), BF)] * 4,
        in_specs=[smem, smem, hbm, hbm, hbm, hbm],
        out_specs=[vmem] * 4,
        scratch_shapes=[
            pltpu.VMEM((2, CAND, MINE), BF),
            pltpu.VMEM((2, 2 * ROWS, MINE), BF),
            pltpu.VMEM((2, 16, PAIR), F32),
            pltpu.VMEM((4, KEYS, PAIR), F32),
            pltpu.VMEM((PAIR, CAND), BF),
            pltpu.VMEM((PAIR, CAND), BF),
            pltpu.VMEM((PAIR, 2 * ROWS), BF),
            pltpu.VMEM((4, KEYS, BLK), F32),
            pltpu.VMEM((4, KEYS, BLK), BF),
            pltpu.VMEM((CAND, PAIR), F32),
            pltpu.VMEM((CAND, PAIR), F32),
            pltpu.VMEM((2, PAIR, BLK), F32),
            pltpu.VMEM((2, PAIR, BLK), F32),
            pltpu.VMEM((2, 2 * ROWS, MINE), BF),
            pltpu.VMEM((2, ROWS, MINE), F32),
            pltpu.VMEM((2, ROWS, MINE), BF),
            pltpu.VMEM((2, ROWS, MINE), BF),
            pltpu.VMEM((2, ROWS, MINE), BF),
            pltpu.VMEM((2, ROWS, MINE), BF),
            pltpu.VMEM((2, ROWS, MINE), BF),
            pltpu.VMEM((4, ROWS, MINE), BF),
            pltpu.VMEM((2, ROWS, MINE), BF),
            pltpu.VMEM((ROWS, MINE), BF),
            pltpu.VMEM((ROWS, MINE), BF),
            pltpu.VMEM((PLANE, PIECE, MINE), BF),
            pltpu.VMEM((PIECE, MINE), F32),
            pltpu.VMEM((8, PIECE, MINE), F32),
            pltpu.VMEM((PIECE, MINE), F32),
            pltpu.VMEM((2 * ROWS, WIDTH), F32),
            dma((4,)), dma, dma, dma((4 * PAIRS,)), dma((4 * PAIRS,)), two, two, two, two,
            dma, dma, dma, dma, dma, dma, dma, dma,
            two, two, two, two, dma((2 * PAIRS,)), dma((2 * PAIRS,)),
            two, two, two, two, two, two, two, two,
        ],
        compiler_params=pltpu.CompilerParams(
            collective_id=0, has_side_effects=True, vmem_limit_bytes=58 * 2**20
        ),
        name="banded",
    )(band, prefix_len, query, keys, values, grad_out)


def solution(mesh):
    rows = P(("outer", "inner"), None)
    return jax.shard_map(
        on_device,
        mesh=mesh,
        in_specs=(rows, rows, rows, rows, rows, P()),
        out_specs=(rows, rows, rows, rows),
        check_vma=False,
    )
```

```python
import functools

import jax
import jax.numpy as jnp
from jax import lax
from jax.experimental import pallas as pl
from jax.experimental.pallas import tpu as pltpu
from jax.sharding import PartitionSpec as P

F32 = jnp.float32
BF = jnp.bfloat16
MESH = pl.DeviceIdType.MESH
BLK = 256
ROWS = 512
WIDTH = 512
PAIR = 128
PAIRS = 2
HEAD = 64
SLOTS = 5
TILES = 7
KEYS = TILES * BLK
CAND = 2560
PROMPT = 2048
MINE = 256
SCALE = HEAD ** -0.5
TO_EXP2 = SCALE * 1.4426950408889634
OFF = -1e30
PLANE = 8
PIECE = 64


def dot_last(a, b):
    return lax.dot_general(a, b, (((1,), (1,)), ((), ())), preferred_element_type=F32)


def dot(a, b):
    return lax.dot_general(a, b, (((1,), (0,)), ((), ())), preferred_element_type=F32)


def at_block(start):
    return pl.ds(pl.multiple_of(start, BLK), BLK)


def fill_bias(listed, plen, bias, base):
    row = lax.broadcasted_iota(jnp.int32, (BLK, PAIR), 0)
    for i in range(4):
        for s in range(SLOTS):
            ok = (base + i - 2 + s) * BLK + row >= plen[0]
            n = (i % 2) * SLOTS + s
            bias[i, s * BLK : (s + 1) * BLK, :] = jnp.where(ok, listed[i // 2, n : n + 1, :], OFF)
        for s in range(2):
            low = (SLOTS + s) * BLK
            bias[i, low : low + BLK, :] = jnp.where(row + s * BLK < plen[0], 0.0, OFF)


def attend(p, u, kv, qg, bias, kt, vt, gt, x, e, dk, dv, att_t, dq_t, result, midway):
    cols = pl.ds(pl.multiple_of(p * PAIR, PAIR), PAIR)
    lane = lax.broadcasted_iota(jnp.int32, (BLK, PAIR), 1)
    combos = [(qb, h) for qb in range(2) for h in range(2)]

    def half(h):
        return (lane < HEAD) if h == 0 else (lane >= HEAD)

    def heads(h):
        return slice(h * HEAD, (h + 1) * HEAD)

    def mine(qb):
        return at_block(u * ROWS + qb * BLK)

    def keys_of(qb, s):
        return at_block(u * ROWS + (qb + s) * BLK) if s < SLOTS else at_block(PROMPT + (s - SLOTS) * BLK)

    qz = [jnp.where(half(h), qg[0, mine(qb), cols], jnp.zeros((), BF)) for qb, h in combos]

    def score(n):
        qb, h = combos[n]
        top = jnp.full((8, BLK), OFF, F32)
        for s in range(TILES):
            t = dot_last(kv[0, keys_of(qb, s), cols], qz[n]) * TO_EXP2
            b = bias[2 * u + qb, s * BLK : (s + 1) * BLK, :]
            t = t + jnp.concatenate([b, b], axis=1)
            x[n, s * BLK : (s + 1) * BLK, :] = t
            top = jnp.maximum(top, jnp.max(t.reshape(BLK // 8, 8, BLK), axis=0))
        return jnp.max(top, axis=0, keepdims=True)

    def weigh(n, top):
        qb, h = combos[n]
        total = jnp.zeros((8, BLK), F32)
        a = jnp.zeros((HEAD, BLK), F32)
        for s in range(TILES):
            expo = jnp.exp2(x[n, s * BLK : (s + 1) * BLK, :] - top)
            total = total + jnp.sum(expo.reshape(BLK // 8, 8, BLK), axis=0)
            eb = expo.astype(BF)
            e[n, s * BLK : (s + 1) * BLK, :] = eb
            a = a + dot(vt[heads(h), keys_of(qb, s)], eb)
        r = 1.0 / jnp.sum(total, axis=0, keepdims=True)
        a = a * r
        att_t[qb, heads(h), :] = a
        r_col = jnp.broadcast_to(r, (PAIR, BLK)).T
        gz = jnp.where(half(h), qg[1, mine(qb), cols].astype(F32) * r_col, 0.0).astype(BF)
        g_row = (gt[heads(h), mine(qb)].astype(F32) * r).astype(BF).astype(F32)
        return gz, jnp.sum(g_row * a, axis=0, keepdims=True)

    def differentiate(n, gz, delta, low, count, rows):
        qb, h = combos[n]
        eb = e[n, low : low + count, :]
        dp = dot_last(kv[1, rows, cols], gz) - delta
        ds = (eb.astype(F32) * dp).astype(BF)
        dv[rows, :] += dot(eb, gz)
        dk[rows, :] += dot(ds, qz[n])
        return dot(kt[heads(h), rows], ds) * SCALE

    def on_prompt(n):
        qb, h = combos[n]
        dq_t[qb, heads(h), :] = differentiate(n, *grads[n], SLOTS * BLK, 2 * BLK, pl.ds(PROMPT, 2 * BLK))

    def on_band(n):
        qb, h = combos[n]
        rows = pl.ds(pl.multiple_of(u * ROWS + qb * BLK, BLK), SLOTS * BLK)
        dq_t[qb, heads(h), :] += differentiate(n, *grads[n], 0, SLOTS * BLK, rows)

    tops = [score(0)]
    grads = []
    for n in range(4):
        if n < 3:
            tops.append(score(n + 1))
        grads.append(weigh(n, tops[n]))
        if n >= 1:
            on_prompt(n - 1)
    on_prompt(3)
    for qb in range(2):
        result[0, mine(qb), cols] = att_t[qb].T.astype(BF)
    midway()
    for n in range(4):
        on_band(n)
    for qb in range(2):
        result[1, mine(qb), cols] = dq_t[qb].T.astype(BF)


def wait_bytes(ref, sem):
    pltpu.make_async_copy(ref, ref, sem).wait()


def kernel(
    band, plen, q, k, v, g, out,
    kv, qg, listed, bias, kt, vt, gt, x, e, dk, dv, att_t, dq_t, result,
    own, near_s, near_r, far_s, far_r, xo, xr, ps, pr, rb, ry, pz, rz, pf, rf,
    local_sem, l_s, l_r, x_s, x_r, e_s, e_r, f_s, f_r,
    b1_s, b1_r, b2_s, b2_r, b3_s, b3_r, b4_s, b4_r,
    n_s, n_r, w_s, w_r, o_s, o_r, r1_s, r1_r, r2_s, r2_r, r3_s, r3_r, r4_s, r4_r,
):
    outer = lax.axis_index("outer")
    inner = lax.axis_index("inner")
    device = outer * 8 + inner
    z = outer // 4
    x_lo = (outer // 2) % 2
    core = outer % 2
    side = inner % 2
    spot = (inner // 2) * 2 + x_lo
    partner = (outer, inner + 1 - 2 * side)
    up = lax.rem(device + 2, 256)
    down = lax.rem(device + 254, 256)
    near = jnp.where(side == 0, down, up)
    far = jnp.where(side == 0, up, down)
    near = (near // 8, near % 8)
    far = (far // 8, far % 8)
    other_core = (outer + 1 - 2 * core, inner)
    root = (0, 0)
    first = device == 0
    bottom = z == 0

    def in_plane(level, at, part, which):
        return ((level * 2 + at % 2) * 2 + which, (at // 2) * 2 + part)

    def in_column(level):
        return ((level * 2 + x_lo) * 2 + core, inner)

    def peer(n):
        return lax.rem(spot + n, PLANE)

    def lanes(part):
        return pl.ds(pl.multiple_of(part * MINE, MINE), MINE)

    def columns(c):
        return pl.ds(pl.multiple_of(c * PAIR, PAIR), PAIR)

    def run(part):
        return pl.ds(pl.multiple_of(part * ROWS, ROWS), ROWS)

    own_rows = run(1 + side)
    near_rows = pl.ds(pl.multiple_of((1 - side) * 3 * ROWS, ROWS), ROWS)
    far_rows = pl.ds(pl.multiple_of(side * 3 * ROWS, ROWS), ROWS)
    held = [(k, kv.at[0], own_rows), (v, kv.at[1], own_rows), (q, qg.at[0], run(side)), (g, qg.at[1], run(side))]
    mine_in = [
        pltpu.make_async_copy(src.at[:, lanes(side)], dst.at[rows], local_sem.at[n])
        for n, (src, dst, rows) in enumerate(held)
    ]
    for c in mine_in:
        c.start()
    for qb in range(2):
        for s in range(SLOTS):
            n = qb * SLOTS + s
            listed[side, n : n + 1, :] = jnp.full((1, PAIR), jnp.where(band[qb, s] >= 0, 0.0, OFF), F32)
    for n in range(2 * SLOTS, 16):
        listed[side, n : n + 1, :] = jnp.zeros((1, PAIR), F32)

    barrier = pltpu.get_barrier_semaphore()

    def hello(target):
        pl.semaphore_signal(barrier, inc=1, device_id=target, device_id_type=MESH)

    for target in (partner, near, far, other_core):
        hello(target)
    for n in range(1, PLANE):
        hello(in_plane(z, peer(n), side, core))

    @pl.when(bottom)
    def _():
        @pl.loop(1, 8)
        def _(n):
            hello(in_column(n))

    @pl.when(jnp.logical_not(bottom))
    def _():
        hello(in_column(0))

    def root_peer(n):
        return in_plane(0, n % PLANE, (n // PLANE) % 2, n // (2 * PLANE))

    @pl.when(first)
    def _():
        @pl.loop(1, 4 * PLANE)
        def _(n):
            hello(root_peer(n))

    @pl.when(jnp.logical_and(bottom, jnp.logical_not(first)))
    def _():
        hello(root)

    greeted = 4 + PLANE - 1 + jnp.where(bottom, 7, 1)
    greeted = greeted + jnp.where(first, 4 * PLANE - 1, jnp.where(bottom, 1, 0))
    for c in mine_in:
        c.wait()
    pl.semaphore_wait(barrier, greeted)

    def send(src, dst, s_sem, r_sem, target):
        return pltpu.make_async_remote_copy(
            src_ref=src, dst_ref=dst, send_sem=s_sem, recv_sem=r_sem,
            device_id=target, device_id_type=MESH,
        )

    def cross(c):
        lane = pl.ds(pl.multiple_of((1 - side) * MINE + c * PAIR, PAIR), PAIR)
        return [
            send(src.at[:, lane], dst.at[rows, columns(c)], x_s.at[4 * c + n], x_r.at[4 * c + n], partner)
            for n, (src, dst, rows) in enumerate(held)
        ]

    def to_near(c):
        return send(
            kv.at[:, own_rows, columns(c)], kv.at[:, near_rows, columns(c)], e_s.at[c], e_r.at[c], near
        )

    def to_far(c):
        return send(
            kv.at[:, run(2 - side), columns(c)], kv.at[:, far_rows, columns(c)], f_s.at[c], f_r.at[c], far
        )

    def strip(at):
        return pl.ds(pl.multiple_of(at * PIECE, PIECE), PIECE)

    def piece(which, at):
        return kv.at[which, pl.ds(pl.multiple_of(PROMPT + at * PIECE, PIECE), PIECE)]

    @pl.when(first)
    def _():
        for which, src, low in ((0, k, 1), (1, v, 0)):

            @pl.loop(low, 2 * PLANE)
            def _(n):
                at = n % PLANE
                send(
                    src.at[strip(at), lanes(n // PLANE)], piece(which, at), b1_s, b1_r,
                    root_peer(n + which * 2 * PLANE),
                ).start()

        own_piece = pltpu.make_async_copy(k.at[strip(0), lanes(0)], piece(0, 0), local_sem.at[0])
        own_piece.start()
        own_piece.wait()

    note = send(listed.at[side], listed.at[side], l_s, l_r, partner)
    note.start()
    for c in cross(0):
        c.start()
    to_near(0).start()

    @pl.when(jnp.logical_and(bottom, jnp.logical_not(first)))
    def _():
        wait_bytes(piece(core, spot), b1_r)

    @pl.when(bottom)
    def _():
        @pl.loop(1, 8)
        def _(n):
            send(piece(core, spot), piece(core, spot), b2_s, b2_r, in_column(n)).start()

    note.wait()
    fill_bias(listed, plen, bias, 2 * (device - side))

    @pl.when(jnp.logical_not(bottom))
    def _():
        wait_bytes(piece(core, spot), b2_r)

    for n in range(1, PLANE):
        send(piece(core, spot), piece(core, spot), b3_s, b3_r, in_plane(z, peer(n), side, core)).start()
    for c, later in zip(cross(0), cross(1)):
        c.wait_send()
        later.start()
    for c in cross(0):
        c.wait_recv()
    to_far(0).start()
    to_near(1).start()
    wait_bytes(kv.at[0, pl.ds(0, (PLANE - 1) * PIECE)], b3_r)
    whole = kv.at[core, pl.ds(PROMPT, ROWS)]
    prompt = send(whole, whole, b4_s, b4_r, other_core)
    prompt.start()
    prompt.wait()

    def near_back(c):
        return send(near_s.at[:, :, columns(c)], near_r.at[:, :, columns(c)], n_s.at[c], n_r.at[c], near)

    def far_back(c):
        return send(far_s.at[:, :, columns(c)], far_r.at[:, :, columns(c)], w_s.at[c], w_r.at[c], far)

    def x_back(c, n):
        if n < 2:
            src, dst = result.at[n, run(1 - side), columns(c)], xr.at[n, :, columns(c)]
        else:
            src, dst = xo.at[:, :, columns(c)], xr.at[2:4, :, columns(c)]
        return send(src, dst, o_s.at[3 * c + n], o_r.at[3 * c + n], partner)

    def swap(c):
        return send(ps.at[1 - core, :, columns(c)], pr.at[:, columns(c)], r1_s.at[c], r1_r.at[c], other_core)

    def scatter(c, n):
        to = peer(n)
        return send(
            rb.at[strip(to), columns(c)], ry.at[spot, :, columns(c)], r2_s.at[c], r2_r.at[c],
            in_plane(z, to, side, core),
        )

    def sink(c):
        return send(pz.at[:, columns(c)], rz.at[z, :, columns(c)], r3_s.at[c], r3_r.at[c], in_column(0))

    def collect(c):
        place = pl.ds(pl.multiple_of(core * ROWS + spot * PIECE, PIECE), PIECE)
        lane = pl.ds(pl.multiple_of(side * MINE + c * PAIR, PAIR), PAIR)
        return send(pf.at[:, columns(c)], rf.at[place, lane], r4_s.at[c], r4_r.at[c], root)

    def hand_prompt(c):
        cols = columns(c)
        for n, grad, scale in ((0, dk, SCALE), (1, dv, 1.0)):
            ps[n, :, cols] = (grad[pl.ds(PROMPT, ROWS), :] * scale).astype(BF)
        swap(c).start()
        x_back(c, 0).start()

    def hand_back(c):
        cols = columns(c)
        reduce_plane(c)
        for n, grad, scale in ((0, dk, SCALE), (1, dv, 1.0)):
            far_s[n, :, cols] = (grad[near_back_rows[1], :] * scale).astype(BF)
        far_back(c).start()
        x_back(c, 1).start()
        near_back(c).wait_recv()
        for n, grad, scale in ((0, dk, SCALE), (1, dv, 1.0)):
            xo[n, :, cols] = (grad[run(2 - side), :] * scale + near_r[n, :, cols].astype(F32)).astype(BF)
        x_back(c, 2).start()
        for n, grad, scale in ((0, dk, SCALE), (1, dv, 1.0)):
            own[n, :, cols] = grad[own_rows, :] * scale

    near_back_rows = (far_rows, near_rows)

    def reduce_plane(c):
        cols = columns(c)
        swap(c).wait_recv()
        rb[:, cols] = (ps[core, :, cols].astype(F32) + pr[:, cols].astype(F32)).astype(BF)
        for n in range(1, PLANE):
            scatter(c, n).start()

    def reduce_column(c):
        cols = columns(c)
        wait_bytes(ry.at[pl.ds(0, PLANE - 1), :, columns(0)], r2_r.at[c])
        ry[spot, :, cols] = rb[strip(spot), cols]
        part = ry[0, :, cols].astype(F32)
        for n in range(1, PLANE):
            part = part + ry[n, :, cols].astype(F32)
        pz[:, cols] = part

        @pl.when(jnp.logical_not(bottom))
        def _():
            sink(c).start()

    def reduce_root(c):
        cols = columns(c)

        @pl.when(bottom)
        def _():
            wait_bytes(rz.at[pl.ds(1, 7), :, columns(0)], r3_r.at[c])
            part = pz[:, cols]
            for n in range(1, 8):
                part = part + rz[n, :, cols]
            pf[:, cols] = part

            @pl.when(first)
            def _():
                rf[pl.ds(0, PIECE), cols] = part

            @pl.when(jnp.logical_not(first))
            def _():
                collect(c).start()

    def settle(c):
        cols = columns(c)
        far_back(c).wait_recv()
        for n in range(2):
            own[n, :, cols] += far_r[n, :, cols].astype(F32)

    @pl.loop(0, 4)
    def _(t):
        p = t // 2
        late = t % 2

        @pl.when(late == 0)
        def _():
            to_near(p).wait_recv()
            dk[...] = jnp.zeros_like(dk)
            dv[...] = jnp.zeros_like(dv)

            to_far(p).wait_recv()
            cols = columns(p)
            kt[...] = kv[0, :, cols].T
            vt[...] = kv[1, :, cols].T
            gt[...] = qg[1, :, cols].T

        u = jnp.where(late == 0, side, 1 - side)

        def midway():
            @pl.when(t == 0)
            def _():
                for c in cross(1):
                    c.wait_recv()
                to_far(1).start()

            for c in range(PAIRS):

                @pl.when(t == 2 * c + 1)
                def _(c=c):
                    hand_prompt(c)

        attend(p, u, kv, qg, bias, kt, vt, gt, x, e, dk, dv, att_t, dq_t, result, midway)

        @pl.when(late == 0)
        def _():
            cols = columns(p)
            for n, grad, scale in ((0, dk, SCALE), (1, dv, 1.0)):
                near_s[n, :, cols] = (grad[near_back_rows[0], :] * scale).astype(BF)
            near_back(p).start()

        @pl.when(t == 1)
        def _():
            hand_back(0)

        @pl.when(t == 2)
        def _():
            reduce_column(0)

        @pl.when(t == 3)
        def _():
            hand_back(1)

    reduce_root(0)
    settle(0)
    reduce_column(1)
    for n in range(2):
        out[n, :, lanes(side)] = result[n, run(side), :]
    settle(1)
    reduce_root(1)
    for c in range(PAIRS):
        for n in range(3):
            x_back(c, n).wait_recv()

    @pl.when(first)
    def _():
        for c in range(PAIRS):
            wait_bytes(rf.at[pl.ds(0, (4 * PLANE - 1) * PIECE // 2), lanes(0)], r4_r.at[c])
        for n in range(2):
            own[n] += rf[pl.ds(n * ROWS, ROWS), lanes(0)]
            xr[2 + n] = (xr[2 + n].astype(F32) + rf[pl.ds(n * ROWS, ROWS), lanes(1)]).astype(BF)

    out[:, :, lanes(1 - side)] = xr[...]
    for n in range(2):
        out[2 + n, :, lanes(side)] = own[n].astype(BF)

    for c in range(PAIRS):
        for copy in cross(1)[: 4 * c] + [x_back(c, n) for n in range(3)]:
            copy.wait_send()
        for copy in (to_near(c), to_far(c), near_back(c), far_back(c), swap(c)):
            copy.wait_send()
        wait_bytes(ry.at[pl.ds(0, PLANE - 1), :, columns(0)], r2_s.at[c])

        @pl.when(jnp.logical_not(bottom))
        def _(c=c):
            sink(c).wait_send()

        @pl.when(jnp.logical_and(bottom, jnp.logical_not(first)))
        def _(c=c):
            collect(c).wait_send()

    wait_bytes(kv.at[0, pl.ds(0, (PLANE - 1) * PIECE)], b3_s)

    @pl.when(bottom)
    def _():
        wait_bytes(kv.at[0, pl.ds(0, 7 * PIECE)], b2_s)

    @pl.when(first)
    def _():
        wait_bytes(kv.at[0, pl.ds(0, (4 * PLANE - 1) * PIECE)], b1_s)


def on_device(query, keys, values, grad_out, band, prefix_len):
    vmem = pl.BlockSpec(memory_space=pltpu.VMEM)
    smem = pl.BlockSpec(memory_space=pltpu.SMEM)
    hbm = pl.BlockSpec(memory_space=pl.ANY)
    dma = pltpu.SemaphoreType.DMA
    two = dma((PAIRS,))
    whole = pl.pallas_call(
        kernel,
        out_shape=jax.ShapeDtypeStruct((4, ROWS, WIDTH), BF),
        in_specs=[smem, smem, hbm, hbm, hbm, hbm],
        out_specs=vmem,
        scratch_shapes=[
            pltpu.VMEM((2, CAND, MINE), BF),
            pltpu.VMEM((2, 2 * ROWS, MINE), BF),
            pltpu.VMEM((2, 16, PAIR), F32),
            pltpu.VMEM((4, KEYS, PAIR), F32),
            pltpu.VMEM((PAIR, CAND), BF),
            pltpu.VMEM((PAIR, CAND), BF),
            pltpu.VMEM((PAIR, 2 * ROWS), BF),
            pltpu.VMEM((4, KEYS, BLK), F32),
            pltpu.VMEM((4, KEYS, BLK), BF),
            pltpu.VMEM((CAND, PAIR), F32),
            pltpu.VMEM((CAND, PAIR), F32),
            pltpu.VMEM((2, PAIR, BLK), F32),
            pltpu.VMEM((2, PAIR, BLK), F32),
            pltpu.VMEM((2, 2 * ROWS, MINE), BF),
            pltpu.VMEM((2, ROWS, MINE), F32),
            pltpu.VMEM((2, ROWS, MINE), BF),
            pltpu.VMEM((2, ROWS, MINE), BF),
            pltpu.VMEM((2, ROWS, MINE), BF),
            pltpu.VMEM((2, ROWS, MINE), BF),
            pltpu.VMEM((2, ROWS, MINE), BF),
            pltpu.VMEM((4, ROWS, MINE), BF),
            pltpu.VMEM((2, ROWS, MINE), BF),
            pltpu.VMEM((ROWS, MINE), BF),
            pltpu.VMEM((ROWS, MINE), BF),
            pltpu.VMEM((PLANE, PIECE, MINE), BF),
            pltpu.VMEM((PIECE, MINE), F32),
            pltpu.VMEM((8, PIECE, MINE), F32),
            pltpu.VMEM((PIECE, MINE), F32),
            pltpu.VMEM((2 * ROWS, WIDTH), F32),
            dma((4,)), dma, dma, dma((4 * PAIRS,)), dma((4 * PAIRS,)), two, two, two, two,
            dma, dma, dma, dma, dma, dma, dma, dma,
            two, two, two, two, dma((3 * PAIRS,)), dma((3 * PAIRS,)),
            two, two, two, two, two, two, two, two,
        ],
        compiler_params=pltpu.CompilerParams(
            collective_id=0, has_side_effects=True, vmem_limit_bytes=58 * 2**20
        ),
        name="banded",
    )(band, prefix_len, query, keys, values, grad_out)
    return tuple(whole[n] for n in range(4))


def solution(mesh):
    rows = P(("outer", "inner"), None)
    return jax.shard_map(
        on_device,
        mesh=mesh,
        in_specs=(rows, rows, rows, rows, rows, P()),
        out_specs=(rows, rows, rows, rows),
        check_vma=False,
    )
```

```python
import functools

import jax
import jax.numpy as jnp
from jax import lax
from jax.experimental import pallas as pl
from jax.experimental.pallas import tpu as pltpu
from jax.sharding import PartitionSpec as P

F32 = jnp.float32
BF = jnp.bfloat16
MESH = pl.DeviceIdType.MESH
BLK = 256
ROWS = 512
WIDTH = 512
PAIR = 128
PAIRS = 2
HEAD = 64
SLOTS = 5
TILES = 7
KEYS = TILES * BLK
CAND = 2560
PROMPT = 2048
MINE = 256
SCALE = HEAD ** -0.5
TO_EXP2 = SCALE * 1.4426950408889634
OFF = -1e30
PLANE = 8
PIECE = 64


def dot_last(a, b):
    return lax.dot_general(a, b, (((1,), (1,)), ((), ())), preferred_element_type=F32)


def dot(a, b):
    return lax.dot_general(a, b, (((1,), (0,)), ((), ())), preferred_element_type=F32)


def at_block(start):
    return pl.ds(pl.multiple_of(start, BLK), BLK)


def fill_bias(listed, plen, bias, base):
    row = lax.broadcasted_iota(jnp.int32, (BLK, PAIR), 0)
    for i in range(4):
        for s in range(SLOTS):
            ok = (base + i - 2 + s) * BLK + row >= plen[0]
            n = (i % 2) * SLOTS + s
            bias[i, s * BLK : (s + 1) * BLK, :] = jnp.where(ok, listed[i // 2, n : n + 1, :], OFF)
        for s in range(2):
            low = (SLOTS + s) * BLK
            bias[i, low : low + BLK, :] = jnp.where(row + s * BLK < plen[0], 0.0, OFF)


def attend(p, u, kv, qg, bias, kt, vt, gt, x, e, dk, dv, att_t, dq_t, result, midway, later):
    cols = pl.ds(pl.multiple_of(p * PAIR, PAIR), PAIR)
    lane = lax.broadcasted_iota(jnp.int32, (BLK, PAIR), 1)
    combos = [(qb, h) for qb in range(2) for h in range(2)]

    def half(h):
        return (lane < HEAD) if h == 0 else (lane >= HEAD)

    def heads(h):
        return slice(h * HEAD, (h + 1) * HEAD)

    def mine(qb):
        return at_block(u * ROWS + qb * BLK)

    def keys_of(qb, s):
        return at_block(u * ROWS + (qb + s) * BLK) if s < SLOTS else at_block(PROMPT + (s - SLOTS) * BLK)

    qz = [jnp.where(half(h), qg[0, mine(qb), cols], jnp.zeros((), BF)) for qb, h in combos]

    def score(n):
        qb, h = combos[n]
        top = jnp.full((8, BLK), OFF, F32)
        for s in range(TILES):
            t = dot_last(kv[0, keys_of(qb, s), cols], qz[n]) * TO_EXP2
            b = bias[2 * u + qb, s * BLK : (s + 1) * BLK, :]
            t = t + jnp.concatenate([b, b], axis=1)
            x[n, s * BLK : (s + 1) * BLK, :] = t
            top = jnp.maximum(top, jnp.max(t.reshape(BLK // 8, 8, BLK), axis=0))
        return jnp.max(top, axis=0, keepdims=True)

    def weigh(n, top):
        qb, h = combos[n]
        total = jnp.zeros((8, BLK), F32)
        a = jnp.zeros((HEAD, BLK), F32)
        for s in range(TILES):
            expo = jnp.exp2(x[n, s * BLK : (s + 1) * BLK, :] - top)
            total = total + jnp.sum(expo.reshape(BLK // 8, 8, BLK), axis=0)
            eb = expo.astype(BF)
            e[n, s * BLK : (s + 1) * BLK, :] = eb
            a = a + dot(vt[heads(h), keys_of(qb, s)], eb)
        r = 1.0 / jnp.sum(total, axis=0, keepdims=True)
        a = a * r
        att_t[qb, heads(h), :] = a
        r_col = jnp.broadcast_to(r, (PAIR, BLK)).T
        gz = jnp.where(half(h), qg[1, mine(qb), cols].astype(F32) * r_col, 0.0).astype(BF)
        g_row = (gt[heads(h), mine(qb)].astype(F32) * r).astype(BF).astype(F32)
        return gz, jnp.sum(g_row * a, axis=0, keepdims=True)

    def differentiate(n, gz, delta, low, count, rows):
        qb, h = combos[n]
        eb = e[n, low : low + count, :]
        dp = dot_last(kv[1, rows, cols], gz) - delta
        ds = (eb.astype(F32) * dp).astype(BF)
        dv[rows, :] += dot(eb, gz)
        dk[rows, :] += dot(ds, qz[n])
        return dot(kt[heads(h), rows], ds) * SCALE

    def on_prompt(n):
        qb, h = combos[n]
        dq_t[qb, heads(h), :] = differentiate(n, *grads[n], SLOTS * BLK, 2 * BLK, pl.ds(PROMPT, 2 * BLK))

    def on_band(n):
        qb, h = combos[n]
        rows = pl.ds(pl.multiple_of(u * ROWS + qb * BLK, BLK), SLOTS * BLK)
        dq_t[qb, heads(h), :] += differentiate(n, *grads[n], 0, SLOTS * BLK, rows)

    tops = [score(0)]
    grads = []
    for n in range(4):
        if n < 3:
            tops.append(score(n + 1))
        grads.append(weigh(n, tops[n]))
        if n >= 1:
            on_prompt(n - 1)
    on_prompt(3)
    for qb in range(2):
        result[0, mine(qb), cols] = att_t[qb].T.astype(BF)
    midway()
    on_band(0)
    on_band(1)
    later()
    on_band(2)
    on_band(3)
    for qb in range(2):
        result[1, mine(qb), cols] = dq_t[qb].T.astype(BF)


def wait_bytes(ref, sem):
    pltpu.make_async_copy(ref, ref, sem).wait()


def kernel(
    band, plen, q, k, v, g, out,
    kv, qg, listed, bias, kt, vt, gt, x, e, dk, dv, att_t, dq_t, result,
    own, near_s, near_r, far_s, far_r, xo, xr, ps, pr, rb, ry, pz, rz, pf, rf,
    local_sem, l_s, l_r, x_s, x_r, e_s, e_r, f_s, f_r,
    b1_s, b1_r, b2_s, b2_r, b3_s, b3_r, b4_s, b4_r,
    n_s, n_r, w_s, w_r, o_s, o_r, r1_s, r1_r, r2_s, r2_r, r3_s, r3_r, r4_s, r4_r,
):
    outer = lax.axis_index("outer")
    inner = lax.axis_index("inner")
    device = outer * 8 + inner
    z = outer // 4
    x_lo = (outer // 2) % 2
    core = outer % 2
    side = inner % 2
    spot = (inner // 2) * 2 + x_lo
    partner = (outer, inner + 1 - 2 * side)
    up = lax.rem(device + 2, 256)
    down = lax.rem(device + 254, 256)
    near = jnp.where(side == 0, down, up)
    far = jnp.where(side == 0, up, down)
    near = (near // 8, near % 8)
    far = (far // 8, far % 8)
    other_core = (outer + 1 - 2 * core, inner)
    root = (0, 0)
    first = device == 0
    bottom = z == 0

    def in_plane(level, at, part, which):
        return ((level * 2 + at % 2) * 2 + which, (at // 2) * 2 + part)

    def in_column(level):
        return ((level * 2 + x_lo) * 2 + core, inner)

    def peer(n):
        return lax.rem(spot + n, PLANE)

    def lanes(part):
        return pl.ds(pl.multiple_of(part * MINE, MINE), MINE)

    def columns(c):
        return pl.ds(pl.multiple_of(c * PAIR, PAIR), PAIR)

    def run(part):
        return pl.ds(pl.multiple_of(part * ROWS, ROWS), ROWS)

    own_rows = run(1 + side)
    near_rows = pl.ds(pl.multiple_of((1 - side) * 3 * ROWS, ROWS), ROWS)
    far_rows = pl.ds(pl.multiple_of(side * 3 * ROWS, ROWS), ROWS)
    held = [(k, kv.at[0], own_rows), (v, kv.at[1], own_rows), (q, qg.at[0], run(side)), (g, qg.at[1], run(side))]
    mine_in = [
        pltpu.make_async_copy(src.at[:, lanes(side)], dst.at[rows], local_sem.at[n])
        for n, (src, dst, rows) in enumerate(held)
    ]
    for c in mine_in:
        c.start()
    for qb in range(2):
        for s in range(SLOTS):
            n = qb * SLOTS + s
            listed[side, n : n + 1, :] = jnp.full((1, PAIR), jnp.where(band[qb, s] >= 0, 0.0, OFF), F32)
    for n in range(2 * SLOTS, 16):
        listed[side, n : n + 1, :] = jnp.zeros((1, PAIR), F32)

    barrier = pltpu.get_barrier_semaphore()

    def hello(target):
        pl.semaphore_signal(barrier, inc=1, device_id=target, device_id_type=MESH)

    for target in (partner, near, far, other_core):
        hello(target)
    for n in range(1, PLANE):
        hello(in_plane(z, peer(n), side, core))

    @pl.when(bottom)
    def _():
        @pl.loop(1, 8)
        def _(n):
            hello(in_column(n))

    @pl.when(jnp.logical_not(bottom))
    def _():
        hello(in_column(0))

    def root_peer(n):
        return in_plane(0, n % PLANE, (n // PLANE) % 2, n // (2 * PLANE))

    @pl.when(first)
    def _():
        @pl.loop(1, 4 * PLANE)
        def _(n):
            hello(root_peer(n))

    @pl.when(jnp.logical_and(bottom, jnp.logical_not(first)))
    def _():
        hello(root)

    greeted = 4 + PLANE - 1 + jnp.where(bottom, 7, 1)
    greeted = greeted + jnp.where(first, 4 * PLANE - 1, jnp.where(bottom, 1, 0))
    for c in mine_in:
        c.wait()
    pl.semaphore_wait(barrier, greeted)

    def send(src, dst, s_sem, r_sem, target):
        return pltpu.make_async_remote_copy(
            src_ref=src, dst_ref=dst, send_sem=s_sem, recv_sem=r_sem,
            device_id=target, device_id_type=MESH,
        )

    def cross(c):
        lane = pl.ds(pl.multiple_of((1 - side) * MINE + c * PAIR, PAIR), PAIR)
        return [
            send(src.at[:, lane], dst.at[rows, columns(c)], x_s.at[4 * c + n], x_r.at[4 * c + n], partner)
            for n, (src, dst, rows) in enumerate(held)
        ]

    def to_near(c):
        return send(
            kv.at[:, own_rows, columns(c)], kv.at[:, near_rows, columns(c)], e_s.at[c], e_r.at[c], near
        )

    def to_far(c):
        return send(
            kv.at[:, run(2 - side), columns(c)], kv.at[:, far_rows, columns(c)], f_s.at[c], f_r.at[c], far
        )

    def strip(at):
        return pl.ds(pl.multiple_of(at * PIECE, PIECE), PIECE)

    def piece(which, at):
        return kv.at[which, pl.ds(pl.multiple_of(PROMPT + at * PIECE, PIECE), PIECE)]

    @pl.when(first)
    def _():
        for which, src, low in ((0, k, 1), (1, v, 0)):

            @pl.loop(low, 2 * PLANE)
            def _(n):
                at = n % PLANE
                send(
                    src.at[strip(at), lanes(n // PLANE)], piece(which, at), b1_s, b1_r,
                    root_peer(n + which * 2 * PLANE),
                ).start()

        own_piece = pltpu.make_async_copy(k.at[strip(0), lanes(0)], piece(0, 0), local_sem.at[0])
        own_piece.start()
        own_piece.wait()

    note = send(listed.at[side], listed.at[side], l_s, l_r, partner)
    note.start()
    groups = [cross(0)[:2], cross(0)[2:], cross(1)[:2], cross(1)[2:]]

    def launch(n):
        for c in groups[n]:
            c.start()

    def sent(n):
        for c in groups[n]:
            c.wait_send()

    def arrived(n):
        for c in groups[n]:
            c.wait_recv()

    launch(0)
    to_near(0).start()

    @pl.when(jnp.logical_and(bottom, jnp.logical_not(first)))
    def _():
        wait_bytes(piece(core, spot), b1_r)

    @pl.when(bottom)
    def _():
        @pl.loop(1, 8)
        def _(n):
            send(piece(core, spot), piece(core, spot), b2_s, b2_r, in_column(n)).start()

    note.wait()
    fill_bias(listed, plen, bias, 2 * (device - side))
    sent(0)
    launch(1)
    arrived(0)
    to_far(0).start()

    @pl.when(jnp.logical_not(bottom))
    def _():
        wait_bytes(piece(core, spot), b2_r)

    for n in range(1, PLANE):
        send(piece(core, spot), piece(core, spot), b3_s, b3_r, in_plane(z, peer(n), side, core)).start()
    sent(1)
    launch(2)
    to_near(1).start()
    wait_bytes(kv.at[0, pl.ds(0, (PLANE - 1) * PIECE)], b3_r)
    whole = kv.at[core, pl.ds(PROMPT, ROWS)]
    prompt = send(whole, whole, b4_s, b4_r, other_core)
    prompt.start()
    arrived(1)
    sent(2)
    launch(3)
    arrived(2)
    to_far(1).start()
    prompt.wait()

    def near_back(c):
        return send(near_s.at[:, :, columns(c)], near_r.at[:, :, columns(c)], n_s.at[c], n_r.at[c], near)

    def far_back(c):
        return send(far_s.at[:, :, columns(c)], far_r.at[:, :, columns(c)], w_s.at[c], w_r.at[c], far)

    def x_back(c, n):
        if n < 2:
            src, dst = result.at[n, run(1 - side), columns(c)], xr.at[n, :, columns(c)]
        else:
            src, dst = xo.at[:, :, columns(c)], xr.at[2:4, :, columns(c)]
        return send(src, dst, o_s.at[3 * c + n], o_r.at[3 * c + n], partner)

    def swap(c):
        return send(ps.at[1 - core, :, columns(c)], pr.at[:, columns(c)], r1_s.at[c], r1_r.at[c], other_core)

    def scatter(c, n):
        to = peer(n)
        return send(
            rb.at[strip(to), columns(c)], ry.at[spot, :, columns(c)], r2_s.at[c], r2_r.at[c],
            in_plane(z, to, side, core),
        )

    def sink(c):
        return send(pz.at[:, columns(c)], rz.at[z, :, columns(c)], r3_s.at[c], r3_r.at[c], in_column(0))

    def collect(c):
        place = pl.ds(pl.multiple_of(core * ROWS + spot * PIECE, PIECE), PIECE)
        lane = pl.ds(pl.multiple_of(side * MINE + c * PAIR, PAIR), PAIR)
        return send(pf.at[:, columns(c)], rf.at[place, lane], r4_s.at[c], r4_r.at[c], root)

    def hand_prompt(c):
        cols = columns(c)
        for n, grad, scale in ((0, dk, SCALE), (1, dv, 1.0)):
            ps[n, :, cols] = (grad[pl.ds(PROMPT, ROWS), :] * scale).astype(BF)
        swap(c).start()
        x_back(c, 0).start()

    def hand_back(c):
        cols = columns(c)
        for n, grad, scale in ((0, dk, SCALE), (1, dv, 1.0)):
            far_s[n, :, cols] = (grad[near_back_rows[1], :] * scale).astype(BF)
        far_back(c).start()
        x_back(c, 1).start()
        near_back(c).wait_recv()
        for n, grad, scale in ((0, dk, SCALE), (1, dv, 1.0)):
            xo[n, :, cols] = (grad[run(2 - side), :] * scale + near_r[n, :, cols].astype(F32)).astype(BF)
        x_back(c, 2).start()
        for n, grad, scale in ((0, dk, SCALE), (1, dv, 1.0)):
            own[n, :, cols] = grad[own_rows, :] * scale

    near_back_rows = (far_rows, near_rows)

    def reduce_plane(c):
        cols = columns(c)
        swap(c).wait_recv()
        rb[:, cols] = (ps[core, :, cols].astype(F32) + pr[:, cols].astype(F32)).astype(BF)
        for n in range(1, PLANE):
            scatter(c, n).start()

    def reduce_column(c):
        cols = columns(c)
        wait_bytes(ry.at[pl.ds(0, PLANE - 1), :, columns(0)], r2_r.at[c])
        ry[spot, :, cols] = rb[strip(spot), cols]
        part = ry[0, :, cols].astype(F32)
        for n in range(1, PLANE):
            part = part + ry[n, :, cols].astype(F32)
        pz[:, cols] = part

        @pl.when(jnp.logical_not(bottom))
        def _():
            sink(c).start()

    def reduce_root(c):
        cols = columns(c)

        @pl.when(bottom)
        def _():
            wait_bytes(rz.at[pl.ds(1, 7), :, columns(0)], r3_r.at[c])
            part = pz[:, cols]
            for n in range(1, 8):
                part = part + rz[n, :, cols]
            pf[:, cols] = part

            @pl.when(first)
            def _():
                rf[pl.ds(0, PIECE), cols] = part

            @pl.when(jnp.logical_not(first))
            def _():
                collect(c).start()

    def settle(c):
        cols = columns(c)
        far_back(c).wait_recv()
        for n in range(2):
            own[n, :, cols] += far_r[n, :, cols].astype(F32)

    @pl.loop(0, 4)
    def _(t):
        p = t // 2
        late = t % 2

        @pl.when(late == 0)
        def _():
            to_near(p).wait_recv()
            dk[...] = jnp.zeros_like(dk)
            dv[...] = jnp.zeros_like(dv)

            to_far(p).wait_recv()

            @pl.when(p == 1)
            def _():
                arrived(3)

            cols = columns(p)
            kt[...] = kv[0, :, cols].T
            vt[...] = kv[1, :, cols].T
            gt[...] = qg[1, :, cols].T

        u = jnp.where(late == 0, side, 1 - side)

        def midway():
            for c in range(PAIRS):

                @pl.when(t == 2 * c + 1)
                def _(c=c):
                    hand_prompt(c)

        def later():
            @pl.when(t == 1)
            def _():
                reduce_plane(0)

            @pl.when(t == 3)
            def _():
                reduce_plane(1)
                reduce_root(0)

        attend(p, u, kv, qg, bias, kt, vt, gt, x, e, dk, dv, att_t, dq_t, result, midway, later)

        @pl.when(late == 0)
        def _():
            cols = columns(p)
            for n, grad, scale in ((0, dk, SCALE), (1, dv, 1.0)):
                near_s[n, :, cols] = (grad[near_back_rows[0], :] * scale).astype(BF)
            near_back(p).start()

        @pl.when(t == 1)
        def _():
            hand_back(0)

        @pl.when(t == 2)
        def _():
            reduce_column(0)

        @pl.when(t == 3)
        def _():
            hand_back(1)

    reduce_column(1)
    reduce_root(1)
    for n in range(2):
        out[n, :, lanes(side)] = result[n, run(side), :]
    settle(0)
    settle(1)
    for c in range(PAIRS):
        for n in range(3):
            x_back(c, n).wait_recv()

    @pl.when(first)
    def _():
        for c in range(PAIRS):
            wait_bytes(rf.at[pl.ds(0, (4 * PLANE - 1) * PIECE // 2), lanes(0)], r4_r.at[c])
        for n in range(2):
            own[n] += rf[pl.ds(n * ROWS, ROWS), lanes(0)]
            xr[2 + n] = (xr[2 + n].astype(F32) + rf[pl.ds(n * ROWS, ROWS), lanes(1)]).astype(BF)

    out[:, :, lanes(1 - side)] = xr[...]
    for n in range(2):
        out[2 + n, :, lanes(side)] = own[n].astype(BF)

    for c in range(PAIRS):
        for copy in (groups[3] if c else []) + [x_back(c, n) for n in range(3)]:
            copy.wait_send()
        for copy in (to_near(c), to_far(c), near_back(c), far_back(c), swap(c)):
            copy.wait_send()
        wait_bytes(ry.at[pl.ds(0, PLANE - 1), :, columns(0)], r2_s.at[c])

        @pl.when(jnp.logical_not(bottom))
        def _(c=c):
            sink(c).wait_send()

        @pl.when(jnp.logical_and(bottom, jnp.logical_not(first)))
        def _(c=c):
            collect(c).wait_send()

    wait_bytes(kv.at[0, pl.ds(0, (PLANE - 1) * PIECE)], b3_s)

    @pl.when(bottom)
    def _():
        wait_bytes(kv.at[0, pl.ds(0, 7 * PIECE)], b2_s)

    @pl.when(first)
    def _():
        wait_bytes(kv.at[0, pl.ds(0, (4 * PLANE - 1) * PIECE)], b1_s)


def on_device(query, keys, values, grad_out, band, prefix_len):
    vmem = pl.BlockSpec(memory_space=pltpu.VMEM)
    smem = pl.BlockSpec(memory_space=pltpu.SMEM)
    hbm = pl.BlockSpec(memory_space=pl.ANY)
    dma = pltpu.SemaphoreType.DMA
    two = dma((PAIRS,))
    whole = pl.pallas_call(
        kernel,
        out_shape=jax.ShapeDtypeStruct((4, ROWS, WIDTH), BF),
        in_specs=[smem, smem, hbm, hbm, hbm, hbm],
        out_specs=vmem,
        scratch_shapes=[
            pltpu.VMEM((2, CAND, MINE), BF),
            pltpu.VMEM((2, 2 * ROWS, MINE), BF),
            pltpu.VMEM((2, 16, PAIR), F32),
            pltpu.VMEM((4, KEYS, PAIR), F32),
            pltpu.VMEM((PAIR, CAND), BF),
            pltpu.VMEM((PAIR, CAND), BF),
            pltpu.VMEM((PAIR, 2 * ROWS), BF),
            pltpu.VMEM((4, KEYS, BLK), F32),
            pltpu.VMEM((4, KEYS, BLK), BF),
            pltpu.VMEM((CAND, PAIR), F32),
            pltpu.VMEM((CAND, PAIR), F32),
            pltpu.VMEM((2, PAIR, BLK), F32),
            pltpu.VMEM((2, PAIR, BLK), F32),
            pltpu.VMEM((2, 2 * ROWS, MINE), BF),
            pltpu.VMEM((2, ROWS, MINE), F32),
            pltpu.VMEM((2, ROWS, MINE), BF),
            pltpu.VMEM((2, ROWS, MINE), BF),
            pltpu.VMEM((2, ROWS, MINE), BF),
            pltpu.VMEM((2, ROWS, MINE), BF),
            pltpu.VMEM((2, ROWS, MINE), BF),
            pltpu.VMEM((4, ROWS, MINE), BF),
            pltpu.VMEM((2, ROWS, MINE), BF),
            pltpu.VMEM((ROWS, MINE), BF),
            pltpu.VMEM((ROWS, MINE), BF),
            pltpu.VMEM((PLANE, PIECE, MINE), BF),
            pltpu.VMEM((PIECE, MINE), F32),
            pltpu.VMEM((8, PIECE, MINE), F32),
            pltpu.VMEM((PIECE, MINE), F32),
            pltpu.VMEM((2 * ROWS, WIDTH), F32),
            dma((4,)), dma, dma, dma((4 * PAIRS,)), dma((4 * PAIRS,)), two, two, two, two,
            dma, dma, dma, dma, dma, dma, dma, dma,
            two, two, two, two, dma((3 * PAIRS,)), dma((3 * PAIRS,)),
            two, two, two, two, two, two, two, two,
        ],
        compiler_params=pltpu.CompilerParams(
            collective_id=0, has_side_effects=True, vmem_limit_bytes=58 * 2**20
        ),
        name="banded",
    )(band, prefix_len, query, keys, values, grad_out)
    return tuple(whole[n] for n in range(4))


def solution(mesh):
    rows = P(("outer", "inner"), None)
    return jax.shard_map(
        on_device,
        mesh=mesh,
        in_specs=(rows, rows, rows, rows, rows, P()),
        out_specs=(rows, rows, rows, rows),
        check_vma=False,
    )
```

```python
import functools

import jax
import jax.numpy as jnp
from jax import lax
from jax.experimental import pallas as pl
from jax.experimental.pallas import tpu as pltpu
from jax.sharding import PartitionSpec as P

F32 = jnp.float32
BF = jnp.bfloat16
MESH = pl.DeviceIdType.MESH
BLK = 256
ROWS = 512
WIDTH = 512
PAIR = 128
PAIRS = 2
HEAD = 64
SLOTS = 5
TILES = 7
KEYS = TILES * BLK
CAND = 2560
PROMPT = 2048
MINE = 256
SCALE = HEAD ** -0.5
TO_EXP2 = SCALE * 1.4426950408889634
OFF = -1e30
PLANE = 8
PIECE = 64


def dot_last(a, b):
    return lax.dot_general(a, b, (((1,), (1,)), ((), ())), preferred_element_type=F32)


def dot(a, b):
    return lax.dot_general(a, b, (((1,), (0,)), ((), ())), preferred_element_type=F32)


def at_block(start):
    return pl.ds(pl.multiple_of(start, BLK), BLK)


def fill_bias(listed, plen, bias, base):
    row = lax.broadcasted_iota(jnp.int32, (BLK, PAIR), 0)
    for i in range(4):
        for s in range(SLOTS):
            ok = (base + i - 2 + s) * BLK + row >= plen[0]
            n = (i % 2) * SLOTS + s
            bias[i, s * BLK : (s + 1) * BLK, :] = jnp.where(ok, listed[i // 2, n : n + 1, :], OFF)
        for s in range(2):
            low = (SLOTS + s) * BLK
            bias[i, low : low + BLK, :] = jnp.where(row + s * BLK < plen[0], 0.0, OFF)


def attend(p, u, kv, qg, bias, kt, vt, gt, x, e, dk, dv, att_t, dq_t, result, midway, later):
    cols = pl.ds(pl.multiple_of(p * PAIR, PAIR), PAIR)
    lane = lax.broadcasted_iota(jnp.int32, (BLK, PAIR), 1)
    combos = [(qb, h) for qb in range(2) for h in range(2)]

    def half(h):
        return (lane < HEAD) if h == 0 else (lane >= HEAD)

    def heads(h):
        return slice(h * HEAD, (h + 1) * HEAD)

    def mine(qb):
        return at_block(u * ROWS + qb * BLK)

    def keys_of(qb, s):
        return at_block(u * ROWS + (qb + s) * BLK) if s < SLOTS else at_block(PROMPT + (s - SLOTS) * BLK)

    qz = [jnp.where(half(h), qg[0, mine(qb), cols], jnp.zeros((), BF)) for qb, h in combos]

    def score(n):
        qb, h = combos[n]
        top = jnp.full((8, BLK), OFF, F32)
        for s in range(TILES):
            t = dot_last(kv[0, keys_of(qb, s), cols], qz[n]) * TO_EXP2
            b = bias[2 * u + qb, s * BLK : (s + 1) * BLK, :]
            t = t + jnp.concatenate([b, b], axis=1)
            x[n, s * BLK : (s + 1) * BLK, :] = t
            top = jnp.maximum(top, jnp.max(t.reshape(BLK // 8, 8, BLK), axis=0))
        return jnp.max(top, axis=0, keepdims=True)

    def weigh(n, top):
        qb, h = combos[n]
        total = jnp.zeros((8, BLK), F32)
        a = jnp.zeros((HEAD, BLK), F32)
        for s in range(TILES):
            expo = jnp.exp2(x[n, s * BLK : (s + 1) * BLK, :] - top)
            total = total + jnp.sum(expo.reshape(BLK // 8, 8, BLK), axis=0)
            eb = expo.astype(BF)
            e[n, s * BLK : (s + 1) * BLK, :] = eb
            a = a + dot(vt[heads(h), keys_of(qb, s)], eb)
        r = 1.0 / jnp.sum(total, axis=0, keepdims=True)
        a = a * r
        att_t[qb, heads(h), :] = a
        r_col = jnp.broadcast_to(r, (PAIR, BLK)).T
        gz = jnp.where(half(h), qg[1, mine(qb), cols].astype(F32) * r_col, 0.0).astype(BF)
        g_row = (gt[heads(h), mine(qb)].astype(F32) * r).astype(BF).astype(F32)
        return gz, jnp.sum(g_row * a, axis=0, keepdims=True)

    def differentiate(n, gz, delta, low, count, rows):
        qb, h = combos[n]
        eb = e[n, low : low + count, :]
        dp = dot_last(kv[1, rows, cols], gz) - delta
        ds = (eb.astype(F32) * dp).astype(BF)
        dv[rows, :] += dot(eb, gz)
        dk[rows, :] += dot(ds, qz[n])
        return dot(kt[heads(h), rows], ds) * SCALE

    def on_prompt(n):
        qb, h = combos[n]
        dq_t[qb, heads(h), :] = differentiate(n, *grads[n], SLOTS * BLK, 2 * BLK, pl.ds(PROMPT, 2 * BLK))

    def on_band(n):
        qb, h = combos[n]
        rows = pl.ds(pl.multiple_of(u * ROWS + qb * BLK, BLK), SLOTS * BLK)
        dq_t[qb, heads(h), :] += differentiate(n, *grads[n], 0, SLOTS * BLK, rows)

    tops = [score(0)]
    grads = []
    for n in range(4):
        if n < 3:
            tops.append(score(n + 1))
        grads.append(weigh(n, tops[n]))
        if n >= 1:
            on_prompt(n - 1)
    on_prompt(3)
    for qb in range(2):
        result[0, mine(qb), cols] = att_t[qb].T.astype(BF)
    midway()
    on_band(0)
    on_band(1)
    result[1, mine(0), cols] = dq_t[0].T.astype(BF)
    later()
    on_band(2)
    on_band(3)
    result[1, mine(1), cols] = dq_t[1].T.astype(BF)


def wait_bytes(ref, sem):
    pltpu.make_async_copy(ref, ref, sem).wait()


def kernel(
    band, plen, q, k, v, g, out,
    kv, qg, listed, bias, kt, vt, gt, x, e, dk, dv, att_t, dq_t, result,
    own, near_s, near_r, far_s, far_r, xo, xr, ps, pr, rb, ry, pz, rz, pf, rf,
    column_sem, local_sem, l_s, l_r, x_s, x_r, e_s, e_r, f_s, f_r,
    stage, b0_s, b0_r, b1_s, b1_r, b2_s, b2_r, b3_s, b3_r, b4_s, b4_r,
    n_s, n_r, w_s, w_r, o_s, o_r, r1_s, r1_r, r2_s, r2_r, r3_s, r3_r, r4_s, r4_r,
):
    outer = lax.axis_index("outer")
    inner = lax.axis_index("inner")
    device = outer * 8 + inner
    z = outer // 4
    x_lo = (outer // 2) % 2
    core = outer % 2
    side = inner % 2
    spot = (inner // 2) * 2 + x_lo
    partner = (outer, inner + 1 - 2 * side)
    up = lax.rem(device + 2, 256)
    down = lax.rem(device + 254, 256)
    near = jnp.where(side == 0, down, up)
    far = jnp.where(side == 0, up, down)
    near = (near // 8, near % 8)
    far = (far // 8, far % 8)
    other_core = (outer + 1 - 2 * core, inner)
    root = (0, 0)
    first = device == 0
    bottom = z == 0
    head = jnp.logical_and(bottom, jnp.logical_and(x_lo == 0, side == 0))
    rest = jnp.logical_and(bottom, jnp.logical_not(jnp.logical_and(x_lo == 0, side == 0)))
    row = inner // 2

    def in_plane(level, at, part, which):
        return ((level * 2 + at % 2) * 2 + which, (at // 2) * 2 + part)

    def in_column(level):
        return ((level * 2 + x_lo) * 2 + core, inner)

    def peer(n):
        return lax.rem(spot + n, PLANE)

    def lanes(part):
        return pl.ds(pl.multiple_of(part * MINE, MINE), MINE)

    def columns(c):
        return pl.ds(pl.multiple_of(c * PAIR, PAIR), PAIR)

    def run(part):
        return pl.ds(pl.multiple_of(part * ROWS, ROWS), ROWS)

    own_rows = run(1 + side)
    near_rows = pl.ds(pl.multiple_of((1 - side) * 3 * ROWS, ROWS), ROWS)
    far_rows = pl.ds(pl.multiple_of(side * 3 * ROWS, ROWS), ROWS)
    held = [(k, kv.at[0], own_rows), (v, kv.at[1], own_rows), (q, qg.at[0], run(side)), (g, qg.at[1], run(side))]
    mine_in = [
        pltpu.make_async_copy(src.at[:, lanes(side)], dst.at[rows], local_sem.at[n])
        for n, (src, dst, rows) in enumerate(held)
    ]
    for c in mine_in:
        c.start()
    for qb in range(2):
        for s in range(SLOTS):
            n = qb * SLOTS + s
            listed[side, n : n + 1, :] = jnp.full((1, PAIR), jnp.where(band[qb, s] >= 0, 0.0, OFF), F32)
    for n in range(2 * SLOTS, 16):
        listed[side, n : n + 1, :] = jnp.zeros((1, PAIR), F32)

    barrier = pltpu.get_barrier_semaphore()

    def hello(target):
        pl.semaphore_signal(barrier, inc=1, device_id=target, device_id_type=MESH)

    for target in (partner, near, far, other_core):
        hello(target)
    for n in range(1, PLANE):
        hello(in_plane(z, peer(n), side, core))

    @pl.when(bottom)
    def _():
        @pl.loop(1, 8)
        def _(n):
            hello(in_column(n))

    def root_peer(n):
        return in_plane(0, n % PLANE, (n // PLANE) % 2, n // (2 * PLANE))

    @pl.when(first)
    def _():
        @pl.loop(1, 4 * PLANE)
        def _(n):
            hello(root_peer(n))

    @pl.when(jnp.logical_and(bottom, jnp.logical_not(first)))
    def _():
        hello(root)

    @pl.when(rest)
    def _():
        hello((core, 2 * row))

    greeted = 4 + PLANE - 1 + jnp.where(bottom, 0, 1)
    greeted = greeted + jnp.where(first, 4 * PLANE - 1, jnp.where(bottom, 1, 0))
    greeted = greeted + jnp.where(head, 3, 0)
    for c in mine_in:
        c.wait()
    pl.semaphore_wait(barrier, greeted)

    @pl.when(jnp.logical_not(bottom))
    def _():
        pl.semaphore_signal(column_sem, inc=1, device_id=in_column(0), device_id_type=MESH)

    def send(src, dst, s_sem, r_sem, target):
        return pltpu.make_async_remote_copy(
            src_ref=src, dst_ref=dst, send_sem=s_sem, recv_sem=r_sem,
            device_id=target, device_id_type=MESH,
        )

    def cross(c):
        lane = pl.ds(pl.multiple_of((1 - side) * MINE + c * PAIR, PAIR), PAIR)
        return [
            send(src.at[:, lane], dst.at[rows, columns(c)], x_s.at[4 * c + n], x_r.at[4 * c + n], partner)
            for n, (src, dst, rows) in enumerate(held)
        ]

    def to_near(c):
        return send(
            kv.at[:, own_rows, columns(c)], kv.at[:, near_rows, columns(c)], e_s.at[c], e_r.at[c], near
        )

    def to_far(c):
        return send(
            kv.at[:, run(2 - side), columns(c)], kv.at[:, far_rows, columns(c)], f_s.at[c], f_r.at[c], far
        )

    def strip(at):
        return pl.ds(pl.multiple_of(at * PIECE, PIECE), PIECE)

    def piece(which, at):
        return kv.at[which, pl.ds(pl.multiple_of(PROMPT + at * PIECE, PIECE), PIECE)]

    quarter = 2 * PIECE

    @pl.when(first)
    def _():
        for which, src, low in ((0, k, 1), (1, v, 0)):

            @pl.loop(low, 4)
            def _(n):
                part = src.at[pl.ds(pl.multiple_of(n * quarter, quarter), quarter)]
                send(part, stage, b0_s, b0_r, (which, 2 * n)).start()

        own_part = pltpu.make_async_copy(k.at[pl.ds(0, quarter)], stage, local_sem.at[0])
        own_part.start()
        own_part.wait()

    note = send(listed.at[side], listed.at[side], l_s, l_r, partner)
    note.start()
    groups = [cross(0)[:2], cross(0)[2:], cross(1)[:2], cross(1)[2:]]

    def launch(n):
        for c in groups[n]:
            c.start()

    def sent(n):
        for c in groups[n]:
            c.wait_send()

    def arrived(n):
        for c in groups[n]:
            c.wait_recv()

    launch(0)
    to_near(0).start()

    @pl.when(jnp.logical_and(head, jnp.logical_not(first)))
    def _():
        wait_bytes(stage, b0_r)

    @pl.when(head)
    def _():
        for n in range(1, 4):
            src = stage.at[pl.ds((n % 2) * PIECE, PIECE), pl.ds((n // 2) * MINE, MINE)]
            at = 2 * row + n % 2
            send(src, piece(core, at), b1_s, b1_r, in_plane(0, at, n // 2, core)).start()
        own_piece = pltpu.make_async_copy(
            stage.at[pl.ds(0, PIECE), pl.ds(0, MINE)], piece(core, spot), local_sem.at[0]
        )
        own_piece.start()
        own_piece.wait()

    @pl.when(rest)
    def _():
        wait_bytes(piece(core, spot), b1_r)

    @pl.when(bottom)
    def _():
        pl.semaphore_wait(column_sem, 7)

        @pl.loop(1, 8)
        def _(n):
            send(piece(core, spot), piece(core, spot), b2_s, b2_r, in_column(n)).start()

    note.wait()
    fill_bias(listed, plen, bias, 2 * (device - side))
    sent(0)
    launch(1)
    arrived(0)
    to_far(0).start()

    @pl.when(jnp.logical_not(bottom))
    def _():
        wait_bytes(piece(core, spot), b2_r)

    for n in range(1, PLANE):
        send(piece(core, spot), piece(core, spot), b3_s, b3_r, in_plane(z, peer(n), side, core)).start()
    sent(1)
    launch(2)
    wait_bytes(kv.at[0, pl.ds(0, (PLANE - 1) * PIECE)], b3_r)
    whole = kv.at[core, pl.ds(PROMPT, ROWS)]
    prompt = send(whole, whole, b4_s, b4_r, other_core)
    prompt.start()
    arrived(1)
    sent(2)
    launch(3)
    arrived(2)
    to_far(1).start()
    prompt.wait()
    to_near(1).start()

    def near_back(c):
        return send(near_s.at[:, :, columns(c)], near_r.at[:, :, columns(c)], n_s.at[c], n_r.at[c], near)

    def far_back(c):
        return send(far_s.at[:, :, columns(c)], far_r.at[:, :, columns(c)], w_s.at[c], w_r.at[c], far)

    def x_back(c, n):
        if n == 0:
            src, dst = result.at[0, run(1 - side), columns(c)], xr.at[0, :, columns(c)]
        elif n < 3:
            rows = at_block((1 - side) * ROWS + (n - 1) * BLK)
            src, dst = result.at[1, rows, columns(c)], xr.at[1, pl.ds((n - 1) * BLK, BLK), columns(c)]
        else:
            src, dst = xo.at[:, :, columns(c)], xr.at[2:4, :, columns(c)]
        return send(src, dst, o_s.at[4 * c + n], o_r.at[4 * c + n], partner)

    def swap(c):
        return send(ps.at[1 - core, :, columns(c)], pr.at[:, columns(c)], r1_s.at[c], r1_r.at[c], other_core)

    def scatter(c, n):
        to = peer(n)
        return send(
            rb.at[strip(to), columns(c)], ry.at[spot, :, columns(c)], r2_s.at[c], r2_r.at[c],
            in_plane(z, to, side, core),
        )

    def sink(c):
        return send(pz.at[:, columns(c)], rz.at[z, :, columns(c)], r3_s.at[c], r3_r.at[c], in_column(0))

    def collect(c):
        place = pl.ds(pl.multiple_of(core * ROWS + spot * PIECE, PIECE), PIECE)
        lane = pl.ds(pl.multiple_of(side * MINE + c * PAIR, PAIR), PAIR)
        return send(pf.at[:, columns(c)], rf.at[place, lane], r4_s.at[c], r4_r.at[c], root)

    def hand_prompt(c):
        cols = columns(c)
        for n, grad, scale in ((0, dk, SCALE), (1, dv, 1.0)):
            ps[n, :, cols] = (grad[pl.ds(PROMPT, ROWS), :] * scale).astype(BF)
        swap(c).start()
        x_back(c, 0).start()

    def hand_back(c):
        cols = columns(c)
        for n, grad, scale in ((0, dk, SCALE), (1, dv, 1.0)):
            far_s[n, :, cols] = (grad[near_back_rows[1], :] * scale).astype(BF)
        far_back(c).start()
        x_back(c, 2).start()
        if c == 1:
            reduce_column(c)
        near_back(c).wait_recv()
        for n, grad, scale in ((0, dk, SCALE), (1, dv, 1.0)):
            xo[n, :, cols] = (grad[run(2 - side), :] * scale + near_r[n, :, cols].astype(F32)).astype(BF)
        x_back(c, 3).start()
        for n, grad, scale in ((0, dk, SCALE), (1, dv, 1.0)):
            own[n, :, cols] = grad[own_rows, :] * scale

    near_back_rows = (far_rows, near_rows)

    def reduce_plane(c):
        cols = columns(c)
        swap(c).wait_recv()
        rb[:, cols] = (ps[core, :, cols].astype(F32) + pr[:, cols].astype(F32)).astype(BF)
        for n in range(1, PLANE):
            scatter(c, n).start()

    def reduce_column(c):
        cols = columns(c)
        wait_bytes(ry.at[pl.ds(0, PLANE - 1), :, columns(0)], r2_r.at[c])
        ry[spot, :, cols] = rb[strip(spot), cols]
        part = ry[0, :, cols].astype(F32)
        for n in range(1, PLANE):
            part = part + ry[n, :, cols].astype(F32)
        pz[:, cols] = part

        @pl.when(jnp.logical_not(bottom))
        def _():
            sink(c).start()

    def reduce_root(c):
        cols = columns(c)

        @pl.when(bottom)
        def _():
            wait_bytes(rz.at[pl.ds(1, 7), :, columns(0)], r3_r.at[c])
            part = pz[:, cols]
            for n in range(1, 8):
                part = part + rz[n, :, cols]
            pf[:, cols] = part

            @pl.when(first)
            def _():
                rf[pl.ds(0, PIECE), cols] = part

            @pl.when(jnp.logical_not(first))
            def _():
                collect(c).start()

    def settle(c):
        cols = columns(c)
        far_back(c).wait_recv()
        for n in range(2):
            own[n, :, cols] += far_r[n, :, cols].astype(F32)

    @pl.loop(0, 4)
    def _(t):
        p = t // 2
        late = t % 2

        @pl.when(late == 0)
        def _():
            to_near(p).wait_recv()
            dk[...] = jnp.zeros_like(dk)
            dv[...] = jnp.zeros_like(dv)

            to_far(p).wait_recv()

            @pl.when(p == 1)
            def _():
                arrived(3)

            cols = columns(p)
            kt[...] = kv[0, :, cols].T
            vt[...] = kv[1, :, cols].T
            gt[...] = qg[1, :, cols].T

        u = jnp.where(late == 0, side, 1 - side)

        def midway():
            for c in range(PAIRS):

                @pl.when(t == 2 * c + 1)
                def _(c=c):
                    hand_prompt(c)

        def later():
            @pl.when(t == 1)
            def _():
                reduce_plane(0)
                x_back(0, 1).start()

            @pl.when(t == 3)
            def _():
                reduce_plane(1)
                x_back(1, 1).start()
                reduce_root(0)

        attend(p, u, kv, qg, bias, kt, vt, gt, x, e, dk, dv, att_t, dq_t, result, midway, later)

        @pl.when(late == 0)
        def _():
            cols = columns(p)
            for n, grad, scale in ((0, dk, SCALE), (1, dv, 1.0)):
                near_s[n, :, cols] = (grad[near_back_rows[0], :] * scale).astype(BF)
            near_back(p).start()

        @pl.when(t == 1)
        def _():
            hand_back(0)

        @pl.when(t == 2)
        def _():
            reduce_column(0)

        @pl.when(t == 3)
        def _():
            hand_back(1)

    reduce_root(1)
    for n in range(2):
        out[n, :, lanes(side)] = result[n, run(side), :]
    settle(0)
    settle(1)
    for c in range(PAIRS):
        for n in range(4):
            x_back(c, n).wait_recv()

    @pl.when(first)
    def _():
        for c in range(PAIRS):
            wait_bytes(rf.at[pl.ds(0, (4 * PLANE - 1) * PIECE // 2), lanes(0)], r4_r.at[c])
        for n in range(2):
            own[n] += rf[pl.ds(n * ROWS, ROWS), lanes(0)]
            xr[2 + n] = (xr[2 + n].astype(F32) + rf[pl.ds(n * ROWS, ROWS), lanes(1)]).astype(BF)

    out[:, :, lanes(1 - side)] = xr[...]
    for n in range(2):
        out[2 + n, :, lanes(side)] = own[n].astype(BF)

    for c in range(PAIRS):
        for copy in (groups[3] if c else []) + [x_back(c, n) for n in range(4)]:
            copy.wait_send()
        for copy in (to_near(c), to_far(c), near_back(c), far_back(c), swap(c)):
            copy.wait_send()
        wait_bytes(ry.at[pl.ds(0, PLANE - 1), :, columns(0)], r2_s.at[c])

        @pl.when(jnp.logical_not(bottom))
        def _(c=c):
            sink(c).wait_send()

        @pl.when(jnp.logical_and(bottom, jnp.logical_not(first)))
        def _(c=c):
            collect(c).wait_send()

    wait_bytes(kv.at[0, pl.ds(0, (PLANE - 1) * PIECE)], b3_s)

    @pl.when(bottom)
    def _():
        wait_bytes(kv.at[0, pl.ds(0, 7 * PIECE)], b2_s)

    @pl.when(head)
    def _():
        wait_bytes(kv.at[0, pl.ds(0, 3 * PIECE)], b1_s)

    @pl.when(first)
    def _():
        wait_bytes(kv.at[0, pl.ds(0, 7 * 2 * quarter)], b0_s)


def on_device(query, keys, values, grad_out, band, prefix_len):
    vmem = pl.BlockSpec(memory_space=pltpu.VMEM)
    smem = pl.BlockSpec(memory_space=pltpu.SMEM)
    hbm = pl.BlockSpec(memory_space=pl.ANY)
    dma = pltpu.SemaphoreType.DMA
    two = dma((PAIRS,))
    whole = pl.pallas_call(
        kernel,
        out_shape=jax.ShapeDtypeStruct((4, ROWS, WIDTH), BF),
        in_specs=[smem, smem, hbm, hbm, hbm, hbm],
        out_specs=vmem,
        scratch_shapes=[
            pltpu.VMEM((2, CAND, MINE), BF),
            pltpu.VMEM((2, 2 * ROWS, MINE), BF),
            pltpu.VMEM((2, 16, PAIR), F32),
            pltpu.VMEM((4, KEYS, PAIR), F32),
            pltpu.VMEM((PAIR, CAND), BF),
            pltpu.VMEM((PAIR, CAND), BF),
            pltpu.VMEM((PAIR, 2 * ROWS), BF),
            pltpu.VMEM((4, KEYS, BLK), F32),
            pltpu.VMEM((4, KEYS, BLK), BF),
            pltpu.VMEM((CAND, PAIR), F32),
            pltpu.VMEM((CAND, PAIR), F32),
            pltpu.VMEM((2, PAIR, BLK), F32),
            pltpu.VMEM((2, PAIR, BLK), F32),
            pltpu.VMEM((2, 2 * ROWS, MINE), BF),
            pltpu.VMEM((2, ROWS, MINE), F32),
            pltpu.VMEM((2, ROWS, MINE), BF),
            pltpu.VMEM((2, ROWS, MINE), BF),
            pltpu.VMEM((2, ROWS, MINE), BF),
            pltpu.VMEM((2, ROWS, MINE), BF),
            pltpu.VMEM((2, ROWS, MINE), BF),
            pltpu.VMEM((4, ROWS, MINE), BF),
            pltpu.VMEM((2, ROWS, MINE), BF),
            pltpu.VMEM((ROWS, MINE), BF),
            pltpu.VMEM((ROWS, MINE), BF),
            pltpu.VMEM((PLANE, PIECE, MINE), BF),
            pltpu.VMEM((PIECE, MINE), F32),
            pltpu.VMEM((8, PIECE, MINE), F32),
            pltpu.VMEM((PIECE, MINE), F32),
            pltpu.VMEM((2 * ROWS, WIDTH), F32),
            pltpu.SemaphoreType.REGULAR,
            dma((4,)), dma, dma, dma((4 * PAIRS,)), dma((4 * PAIRS,)), two, two, two, two,
            pltpu.VMEM((2 * PIECE, WIDTH), BF), dma, dma,
            dma, dma, dma, dma, dma, dma, dma, dma,
            two, two, two, two, dma((4 * PAIRS,)), dma((4 * PAIRS,)),
            two, two, two, two, two, two, two, two,
        ],
        compiler_params=pltpu.CompilerParams(
            collective_id=0, has_side_effects=True, vmem_limit_bytes=58 * 2**20
        ),
        name="banded",
    )(band, prefix_len, query, keys, values, grad_out)
    return tuple(whole[n] for n in range(4))


def solution(mesh):
    rows = P(("outer", "inner"), None)
    return jax.shard_map(
        on_device,
        mesh=mesh,
        in_specs=(rows, rows, rows, rows, rows, P()),
        out_specs=(rows, rows, rows, rows),
        check_vma=False,
    )
```

```python
import functools

import jax
import jax.numpy as jnp
from jax import lax
from jax.experimental import pallas as pl
from jax.experimental.pallas import tpu as pltpu
from jax.sharding import PartitionSpec as P

F32 = jnp.float32
BF = jnp.bfloat16
MESH = pl.DeviceIdType.MESH
BLK = 256
ROWS = 512
WIDTH = 512
PAIR = 128
PAIRS = 2
HEAD = 64
SLOTS = 5
TILES = 7
KEYS = TILES * BLK
CAND = 2560
PROMPT = 2048
MINE = 256
SCALE = HEAD ** -0.5
TO_EXP2 = SCALE * 1.4426950408889634
OFF = -1e30
PLANE = 8
PIECE = 64


def dot_last(a, b):
    return lax.dot_general(a, b, (((1,), (1,)), ((), ())), preferred_element_type=F32)


def dot(a, b):
    return lax.dot_general(a, b, (((1,), (0,)), ((), ())), preferred_element_type=F32)


def at_block(start):
    return pl.ds(pl.multiple_of(start, BLK), BLK)


def fill_bias(listed, plen, bias, base):
    row = lax.broadcasted_iota(jnp.int32, (BLK, PAIR), 0)
    for i in range(4):
        for s in range(SLOTS):
            ok = (base + i - 2 + s) * BLK + row >= plen[0]
            n = (i % 2) * SLOTS + s
            bias[i, s * BLK : (s + 1) * BLK, :] = jnp.where(ok, listed[i // 2, n : n + 1, :], OFF)
        for s in range(2):
            low = (SLOTS + s) * BLK
            bias[i, low : low + BLK, :] = jnp.where(row + s * BLK < plen[0], 0.0, OFF)


def attend(p, u, kv, qg, bias, kt, vt, gt, x, e, dk, dv, att_t, dq_t, result, midway, later):
    cols = pl.ds(pl.multiple_of(p * PAIR, PAIR), PAIR)
    lane = lax.broadcasted_iota(jnp.int32, (BLK, PAIR), 1)
    combos = [(qb, h) for qb in range(2) for h in range(2)]

    def half(h):
        return (lane < HEAD) if h == 0 else (lane >= HEAD)

    def heads(h):
        return slice(h * HEAD, (h + 1) * HEAD)

    def mine(qb):
        return at_block(u * ROWS + qb * BLK)

    def keys_of(qb, s):
        return at_block(u * ROWS + (qb + s) * BLK) if s < SLOTS else at_block(PROMPT + (s - SLOTS) * BLK)

    qz = [jnp.where(half(h), qg[0, mine(qb), cols], jnp.zeros((), BF)) for qb, h in combos]

    def score(n):
        qb, h = combos[n]
        top = jnp.full((8, BLK), OFF, F32)
        for s in range(TILES):
            t = dot_last(kv[0, keys_of(qb, s), cols], qz[n]) * TO_EXP2
            b = bias[2 * u + qb, s * BLK : (s + 1) * BLK, :]
            t = t + jnp.concatenate([b, b], axis=1)
            x[n, s * BLK : (s + 1) * BLK, :] = t
            top = jnp.maximum(top, jnp.max(t.reshape(BLK // 8, 8, BLK), axis=0))
        return jnp.max(top, axis=0, keepdims=True)

    def weigh(n, top):
        qb, h = combos[n]
        total = jnp.zeros((8, BLK), F32)
        a = jnp.zeros((HEAD, BLK), F32)
        for s in range(TILES):
            expo = jnp.exp2(x[n, s * BLK : (s + 1) * BLK, :] - top)
            total = total + jnp.sum(expo.reshape(BLK // 8, 8, BLK), axis=0)
            eb = expo.astype(BF)
            e[n, s * BLK : (s + 1) * BLK, :] = eb
            a = a + dot(vt[heads(h), keys_of(qb, s)], eb)
        r = 1.0 / jnp.sum(total, axis=0, keepdims=True)
        a = a * r
        att_t[qb, heads(h), :] = a
        r_col = jnp.broadcast_to(r, (PAIR, BLK)).T
        gz = jnp.where(half(h), qg[1, mine(qb), cols].astype(F32) * r_col, 0.0).astype(BF)
        g_row = (gt[heads(h), mine(qb)].astype(F32) * r).astype(BF).astype(F32)
        return gz, jnp.sum(g_row * a, axis=0, keepdims=True)

    def differentiate(n, gz, delta, low, count, rows):
        qb, h = combos[n]
        eb = e[n, low : low + count, :]
        dp = dot_last(kv[1, rows, cols], gz) - delta
        ds = (eb.astype(F32) * dp).astype(BF)
        dv[rows, :] += dot(eb, gz)
        dk[rows, :] += dot(ds, qz[n])
        return dot(kt[heads(h), rows], ds) * SCALE

    def on_prompt(n):
        qb, h = combos[n]
        dq_t[qb, heads(h), :] = differentiate(n, *grads[n], SLOTS * BLK, 2 * BLK, pl.ds(PROMPT, 2 * BLK))

    def on_band(n):
        qb, h = combos[n]
        rows = pl.ds(pl.multiple_of(u * ROWS + qb * BLK, BLK), SLOTS * BLK)
        dq_t[qb, heads(h), :] += differentiate(n, *grads[n], 0, SLOTS * BLK, rows)

    tops = [score(0)]
    grads = []
    for n in range(4):
        if n < 3:
            tops.append(score(n + 1))
        grads.append(weigh(n, tops[n]))
        if n >= 1:
            on_prompt(n - 1)
    on_prompt(3)
    for qb in range(2):
        result[0, mine(qb), cols] = att_t[qb].T.astype(BF)
    midway()
    on_band(0)
    on_band(1)
    result[1, mine(0), cols] = dq_t[0].T.astype(BF)
    later()
    on_band(2)
    on_band(3)
    result[1, mine(1), cols] = dq_t[1].T.astype(BF)


def wait_bytes(ref, sem):
    pltpu.make_async_copy(ref, ref, sem).wait()


def kernel(
    band, plen, q, k, v, g, out,
    kv, qg, listed, bias, kt, vt, gt, x, e, dk, dv, att_t, dq_t, result,
    own, near_s, near_r, far_s, far_r, xo, xr, ps, pr, rb, ry, pz, rz, pf, rf,
    column_sem, local_sem, l_s, l_r, x_s, x_r, e_s, e_r, f_s, f_r,
    stage, b0_s, b0_r, b1_s, b1_r, b2_s, b2_r, b3_s, b3_r, b4_s, b4_r,
    n_s, n_r, w_s, w_r, o_s, o_r, r1_s, r1_r, r2_s, r2_r, r3_s, r3_r, r4_s, r4_r,
):
    outer = lax.axis_index("outer")
    inner = lax.axis_index("inner")
    device = outer * 8 + inner
    z = outer // 4
    x_lo = (outer // 2) % 2
    core = outer % 2
    side = inner % 2
    spot = (inner // 2) * 2 + x_lo
    partner = (outer, inner + 1 - 2 * side)
    up = lax.rem(device + 2, 256)
    down = lax.rem(device + 254, 256)
    near = jnp.where(side == 0, down, up)
    far = jnp.where(side == 0, up, down)
    near = (near // 8, near % 8)
    far = (far // 8, far % 8)
    other_core = (outer + 1 - 2 * core, inner)
    root = (0, 0)
    first = device == 0
    bottom = z == 0
    head = jnp.logical_and(bottom, jnp.logical_and(x_lo == 0, side == 0))
    rest = jnp.logical_and(bottom, jnp.logical_not(jnp.logical_and(x_lo == 0, side == 0)))
    row = inner // 2

    def in_plane(level, at, part, which):
        return ((level * 2 + at % 2) * 2 + which, (at // 2) * 2 + part)

    def in_column(level):
        return ((level * 2 + x_lo) * 2 + core, inner)

    def peer(n):
        return lax.rem(spot + n, PLANE)

    def lanes(part):
        return pl.ds(pl.multiple_of(part * MINE, MINE), MINE)

    def columns(c):
        return pl.ds(pl.multiple_of(c * PAIR, PAIR), PAIR)

    def run(part):
        return pl.ds(pl.multiple_of(part * ROWS, ROWS), ROWS)

    own_rows = run(1 + side)
    near_rows = pl.ds(pl.multiple_of((1 - side) * 3 * ROWS, ROWS), ROWS)
    far_rows = pl.ds(pl.multiple_of(side * 3 * ROWS, ROWS), ROWS)
    held = [(k, kv.at[0], own_rows), (v, kv.at[1], own_rows), (q, qg.at[0], run(side)), (g, qg.at[1], run(side))]
    mine_in = [
        pltpu.make_async_copy(src.at[:, lanes(side)], dst.at[rows], local_sem.at[n])
        for n, (src, dst, rows) in enumerate(held)
    ]
    for c in mine_in:
        c.start()
    for qb in range(2):
        for s in range(SLOTS):
            n = qb * SLOTS + s
            listed[side, n : n + 1, :] = jnp.full((1, PAIR), jnp.where(band[qb, s] >= 0, 0.0, OFF), F32)
    for n in range(2 * SLOTS, 16):
        listed[side, n : n + 1, :] = jnp.zeros((1, PAIR), F32)

    barrier = pltpu.get_barrier_semaphore()

    def hello(target):
        pl.semaphore_signal(barrier, inc=1, device_id=target, device_id_type=MESH)

    for target in (partner, near, far, other_core):
        hello(target)
    for n in range(1, PLANE):
        hello(in_plane(z, peer(n), side, core))

    @pl.when(bottom)
    def _():
        @pl.loop(1, 8)
        def _(n):
            hello(in_column(n))

    def root_peer(n):
        return in_plane(0, n % PLANE, (n // PLANE) % 2, n // (2 * PLANE))

    @pl.when(first)
    def _():
        @pl.loop(1, 4 * PLANE)
        def _(n):
            hello(root_peer(n))

    @pl.when(jnp.logical_and(bottom, jnp.logical_not(first)))
    def _():
        hello(root)

    @pl.when(rest)
    def _():
        hello((core, 2 * row))

    greeted = 4 + PLANE - 1 + jnp.where(bottom, 0, 1)
    greeted = greeted + jnp.where(first, 4 * PLANE - 1, jnp.where(bottom, 1, 0))
    greeted = greeted + jnp.where(head, 3, 0)
    for c in mine_in:
        c.wait()
    pl.semaphore_wait(barrier, greeted)

    @pl.when(jnp.logical_not(bottom))
    def _():
        pl.semaphore_signal(column_sem, inc=1, device_id=in_column(0), device_id_type=MESH)

    def send(src, dst, s_sem, r_sem, target):
        return pltpu.make_async_remote_copy(
            src_ref=src, dst_ref=dst, send_sem=s_sem, recv_sem=r_sem,
            device_id=target, device_id_type=MESH,
        )

    def cross(c):
        lane = pl.ds(pl.multiple_of((1 - side) * MINE + c * PAIR, PAIR), PAIR)
        return [
            send(src.at[:, lane], dst.at[rows, columns(c)], x_s.at[4 * c + n], x_r.at[4 * c + n], partner)
            for n, (src, dst, rows) in enumerate(held)
        ]

    def to_near(c):
        return send(
            kv.at[:, own_rows, columns(c)], kv.at[:, near_rows, columns(c)], e_s.at[c], e_r.at[c], near
        )

    def to_far(c):
        return send(
            kv.at[:, run(2 - side), columns(c)], kv.at[:, far_rows, columns(c)], f_s.at[c], f_r.at[c], far
        )

    def strip(at):
        return pl.ds(pl.multiple_of(at * PIECE, PIECE), PIECE)

    def piece(which, at):
        return kv.at[which, pl.ds(pl.multiple_of(PROMPT + at * PIECE, PIECE), PIECE)]

    quarter = 2 * PIECE

    @pl.when(first)
    def _():
        for which, src, low in ((0, k, 1), (1, v, 0)):

            @pl.loop(low, 4)
            def _(n):
                part = src.at[pl.ds(pl.multiple_of(n * quarter, quarter), quarter)]
                send(part, stage, b0_s, b0_r, (which, 2 * n)).start()

        own_part = pltpu.make_async_copy(k.at[pl.ds(0, quarter)], stage, local_sem.at[0])
        own_part.start()
        own_part.wait()

    note = send(listed.at[side], listed.at[side], l_s, l_r, partner)
    note.start()
    groups = [cross(0)[:2], cross(0)[2:], cross(1)[:2], cross(1)[2:]]

    def launch(n):
        for c in groups[n]:
            c.start()

    def sent(n):
        for c in groups[n]:
            c.wait_send()

    def arrived(n):
        for c in groups[n]:
            c.wait_recv()

    launch(0)
    to_near(0).start()

    @pl.when(jnp.logical_and(head, jnp.logical_not(first)))
    def _():
        wait_bytes(stage, b0_r)

    @pl.when(head)
    def _():
        for n in range(1, 4):
            src = stage.at[pl.ds((n % 2) * PIECE, PIECE), pl.ds((n // 2) * MINE, MINE)]
            at = 2 * row + n % 2
            send(src, piece(core, at), b1_s, b1_r, in_plane(0, at, n // 2, core)).start()
        own_piece = pltpu.make_async_copy(
            stage.at[pl.ds(0, PIECE), pl.ds(0, MINE)], piece(core, spot), local_sem.at[0]
        )
        own_piece.start()
        own_piece.wait()

    @pl.when(rest)
    def _():
        wait_bytes(piece(core, spot), b1_r)

    @pl.when(bottom)
    def _():
        pl.semaphore_wait(column_sem, 7)

        @pl.loop(1, 8)
        def _(n):
            send(piece(core, spot), piece(core, spot), b2_s, b2_r, in_column(n)).start()

    note.wait()
    fill_bias(listed, plen, bias, 2 * (device - side))
    sent(0)
    launch(1)
    arrived(0)
    to_far(0).start()

    @pl.when(jnp.logical_not(bottom))
    def _():
        wait_bytes(piece(core, spot), b2_r)

    for n in range(1, PLANE):
        send(piece(core, spot), piece(core, spot), b3_s, b3_r, in_plane(z, peer(n), side, core)).start()
    sent(1)
    launch(2)
    wait_bytes(kv.at[0, pl.ds(0, (PLANE - 1) * PIECE)], b3_r)
    whole = kv.at[core, pl.ds(PROMPT, ROWS)]
    prompt = send(whole, whole, b4_s, b4_r, other_core)
    prompt.start()
    arrived(1)
    arrived(2)
    to_far(1).start()
    prompt.wait()
    sent(2)
    launch(3)
    to_near(1).start()

    def near_back(c):
        return send(near_s.at[:, :, columns(c)], near_r.at[:, :, columns(c)], n_s.at[c], n_r.at[c], near)

    def far_back(c):
        return send(far_s.at[:, :, columns(c)], far_r.at[:, :, columns(c)], w_s.at[c], w_r.at[c], far)

    def x_back(c, n):
        if n == 0:
            src, dst = result.at[0, run(1 - side), columns(c)], xr.at[0, :, columns(c)]
        elif n < 3:
            rows = at_block((1 - side) * ROWS + (n - 1) * BLK)
            src, dst = result.at[1, rows, columns(c)], xr.at[1, pl.ds((n - 1) * BLK, BLK), columns(c)]
        else:
            src, dst = xo.at[:, :, columns(c)], xr.at[2:4, :, columns(c)]
        return send(src, dst, o_s.at[4 * c + n], o_r.at[4 * c + n], partner)

    def swap(c):
        return send(ps.at[1 - core, :, columns(c)], pr.at[:, columns(c)], r1_s.at[c], r1_r.at[c], other_core)

    def scatter(c, n):
        to = peer(n)
        return send(
            rb.at[strip(to), columns(c)], ry.at[spot, :, columns(c)], r2_s.at[c], r2_r.at[c],
            in_plane(z, to, side, core),
        )

    def sink(c):
        return send(pz.at[:, columns(c)], rz.at[z, :, columns(c)], r3_s.at[c], r3_r.at[c], in_column(0))

    def collect(c):
        place = pl.ds(pl.multiple_of(core * ROWS + spot * PIECE, PIECE), PIECE)
        lane = pl.ds(pl.multiple_of(side * MINE + c * PAIR, PAIR), PAIR)
        return send(pf.at[:, columns(c)], rf.at[place, lane], r4_s.at[c], r4_r.at[c], root)

    def hand_prompt(c):
        cols = columns(c)
        for n, grad, scale in ((0, dk, SCALE), (1, dv, 1.0)):
            ps[n, :, cols] = (grad[pl.ds(PROMPT, ROWS), :] * scale).astype(BF)
        swap(c).start()
        x_back(c, 0).start()

    def hand_back(c):
        cols = columns(c)
        for n, grad, scale in ((0, dk, SCALE), (1, dv, 1.0)):
            far_s[n, :, cols] = (grad[near_back_rows[1], :] * scale).astype(BF)
        far_back(c).start()
        x_back(c, 2).start()
        if c == 1:
            reduce_column(c)
        near_back(c).wait_recv()
        for n, grad, scale in ((0, dk, SCALE), (1, dv, 1.0)):
            xo[n, :, cols] = (grad[run(2 - side), :] * scale + near_r[n, :, cols].astype(F32)).astype(BF)
        x_back(c, 3).start()
        for n, grad, scale in ((0, dk, SCALE), (1, dv, 1.0)):
            own[n, :, cols] = grad[own_rows, :] * scale

    near_back_rows = (far_rows, near_rows)

    def reduce_plane(c):
        cols = columns(c)
        swap(c).wait_recv()
        rb[:, cols] = (ps[core, :, cols].astype(F32) + pr[:, cols].astype(F32)).astype(BF)
        for n in range(1, PLANE):
            scatter(c, n).start()

    def reduce_column(c):
        cols = columns(c)
        wait_bytes(ry.at[pl.ds(0, PLANE - 1), :, columns(0)], r2_r.at[c])
        ry[spot, :, cols] = rb[strip(spot), cols]
        part = ry[0, :, cols].astype(F32)
        for n in range(1, PLANE):
            part = part + ry[n, :, cols].astype(F32)
        pz[:, cols] = part

        @pl.when(jnp.logical_not(bottom))
        def _():
            sink(c).start()

    def reduce_root(c):
        cols = columns(c)

        @pl.when(bottom)
        def _():
            wait_bytes(rz.at[pl.ds(1, 7), :, columns(0)], r3_r.at[c])
            part = pz[:, cols]
            for n in range(1, 8):
                part = part + rz[n, :, cols]
            pf[:, cols] = part

            @pl.when(first)
            def _():
                rf[pl.ds(0, PIECE), cols] = part

            @pl.when(jnp.logical_not(first))
            def _():
                collect(c).start()

    def settle(c):
        cols = columns(c)
        far_back(c).wait_recv()
        for n in range(2):
            own[n, :, cols] += far_r[n, :, cols].astype(F32)

    @pl.loop(0, 4)
    def _(t):
        p = t // 2
        late = t % 2

        @pl.when(late == 0)
        def _():
            to_near(p).wait_recv()
            dk[...] = jnp.zeros_like(dk)
            dv[...] = jnp.zeros_like(dv)

            to_far(p).wait_recv()

            @pl.when(p == 1)
            def _():
                arrived(3)

            cols = columns(p)
            kt[...] = kv[0, :, cols].T
            vt[...] = kv[1, :, cols].T
            gt[...] = qg[1, :, cols].T

        u = jnp.where(late == 0, side, 1 - side)

        def midway():
            for c in range(PAIRS):

                @pl.when(t == 2 * c + 1)
                def _(c=c):
                    hand_prompt(c)

        def later():
            @pl.when(t == 1)
            def _():
                reduce_plane(0)
                x_back(0, 1).start()

            @pl.when(t == 3)
            def _():
                reduce_plane(1)
                x_back(1, 1).start()
                reduce_root(0)

        attend(p, u, kv, qg, bias, kt, vt, gt, x, e, dk, dv, att_t, dq_t, result, midway, later)

        @pl.when(late == 0)
        def _():
            cols = columns(p)
            for n, grad, scale in ((0, dk, SCALE), (1, dv, 1.0)):
                near_s[n, :, cols] = (grad[near_back_rows[0], :] * scale).astype(BF)
            near_back(p).start()

        @pl.when(t == 1)
        def _():
            hand_back(0)

        @pl.when(t == 2)
        def _():
            reduce_column(0)

        @pl.when(t == 3)
        def _():
            hand_back(1)

    reduce_root(1)
    for n in range(2):
        out[n, :, lanes(side)] = result[n, run(side), :]
    settle(0)
    settle(1)
    for c in range(PAIRS):
        for n in range(4):
            x_back(c, n).wait_recv()

    @pl.when(first)
    def _():
        for c in range(PAIRS):
            wait_bytes(rf.at[pl.ds(0, (4 * PLANE - 1) * PIECE // 2), lanes(0)], r4_r.at[c])
        for n in range(2):
            own[n] += rf[pl.ds(n * ROWS, ROWS), lanes(0)]
            xr[2 + n] = (xr[2 + n].astype(F32) + rf[pl.ds(n * ROWS, ROWS), lanes(1)]).astype(BF)

    out[:, :, lanes(1 - side)] = xr[...]
    for n in range(2):
        out[2 + n, :, lanes(side)] = own[n].astype(BF)

    for c in range(PAIRS):
        for copy in (groups[3] if c else []) + [x_back(c, n) for n in range(4)]:
            copy.wait_send()
        for copy in (to_near(c), to_far(c), near_back(c), far_back(c), swap(c)):
            copy.wait_send()
        wait_bytes(ry.at[pl.ds(0, PLANE - 1), :, columns(0)], r2_s.at[c])

        @pl.when(jnp.logical_not(bottom))
        def _(c=c):
            sink(c).wait_send()

        @pl.when(jnp.logical_and(bottom, jnp.logical_not(first)))
        def _(c=c):
            collect(c).wait_send()

    wait_bytes(kv.at[0, pl.ds(0, (PLANE - 1) * PIECE)], b3_s)

    @pl.when(bottom)
    def _():
        wait_bytes(kv.at[0, pl.ds(0, 7 * PIECE)], b2_s)

    @pl.when(head)
    def _():
        wait_bytes(kv.at[0, pl.ds(0, 3 * PIECE)], b1_s)

    @pl.when(first)
    def _():
        wait_bytes(kv.at[0, pl.ds(0, 7 * 2 * quarter)], b0_s)


def on_device(query, keys, values, grad_out, band, prefix_len):
    vmem = pl.BlockSpec(memory_space=pltpu.VMEM)
    smem = pl.BlockSpec(memory_space=pltpu.SMEM)
    hbm = pl.BlockSpec(memory_space=pl.ANY)
    dma = pltpu.SemaphoreType.DMA
    two = dma((PAIRS,))
    whole = pl.pallas_call(
        kernel,
        out_shape=jax.ShapeDtypeStruct((4, ROWS, WIDTH), BF),
        in_specs=[smem, smem, hbm, hbm, hbm, hbm],
        out_specs=vmem,
        scratch_shapes=[
            pltpu.VMEM((2, CAND, MINE), BF),
            pltpu.VMEM((2, 2 * ROWS, MINE), BF),
            pltpu.VMEM((2, 16, PAIR), F32),
            pltpu.VMEM((4, KEYS, PAIR), F32),
            pltpu.VMEM((PAIR, CAND), BF),
            pltpu.VMEM((PAIR, CAND), BF),
            pltpu.VMEM((PAIR, 2 * ROWS), BF),
            pltpu.VMEM((4, KEYS, BLK), F32),
            pltpu.VMEM((4, KEYS, BLK), BF),
            pltpu.VMEM((CAND, PAIR), F32),
            pltpu.VMEM((CAND, PAIR), F32),
            pltpu.VMEM((2, PAIR, BLK), F32),
            pltpu.VMEM((2, PAIR, BLK), F32),
            pltpu.VMEM((2, 2 * ROWS, MINE), BF),
            pltpu.VMEM((2, ROWS, MINE), F32),
            pltpu.VMEM((2, ROWS, MINE), BF),
            pltpu.VMEM((2, ROWS, MINE), BF),
            pltpu.VMEM((2, ROWS, MINE), BF),
            pltpu.VMEM((2, ROWS, MINE), BF),
            pltpu.VMEM((2, ROWS, MINE), BF),
            pltpu.VMEM((4, ROWS, MINE), BF),
            pltpu.VMEM((2, ROWS, MINE), BF),
            pltpu.VMEM((ROWS, MINE), BF),
            pltpu.VMEM((ROWS, MINE), BF),
            pltpu.VMEM((PLANE, PIECE, MINE), BF),
            pltpu.VMEM((PIECE, MINE), F32),
            pltpu.VMEM((8, PIECE, MINE), F32),
            pltpu.VMEM((PIECE, MINE), F32),
            pltpu.VMEM((2 * ROWS, WIDTH), F32),
            pltpu.SemaphoreType.REGULAR,
            dma((4,)), dma, dma, dma((4 * PAIRS,)), dma((4 * PAIRS,)), two, two, two, two,
            pltpu.VMEM((2 * PIECE, WIDTH), BF), dma, dma,
            dma, dma, dma, dma, dma, dma, dma, dma,
            two, two, two, two, dma((4 * PAIRS,)), dma((4 * PAIRS,)),
            two, two, two, two, two, two, two, two,
        ],
        compiler_params=pltpu.CompilerParams(
            collective_id=0, has_side_effects=True, vmem_limit_bytes=58 * 2**20
        ),
        name="banded",
    )(band, prefix_len, query, keys, values, grad_out)
    return tuple(whole[n] for n in range(4))


def solution(mesh):
    rows = P(("outer", "inner"), None)
    return jax.shard_map(
        on_device,
        mesh=mesh,
        in_specs=(rows, rows, rows, rows, rows, P()),
        out_specs=(rows, rows, rows, rows),
        check_vma=False,
    )
```
